32 devices in a mesh: gz: 4 (over y, core), xy: 8 (over z, x).
Axes of the slice: x: 2, y: 2, z: 4, core: 2. Of those that a mesh axis runs over, the one named last changes fastest.
Arguments:
- right_side: float32 [12, 8, 16, 512], P(None, 'gz', 'xy'), may hold values from -24 to 24
- jac_diag: bfloat16 [12, 12, 8, 16, 512], P(None, None, 'gz', 'xy'), may hold values from -1.25 to 7.05
- jac_off: bfloat16 [6, 12, 12, 8, 16, 512], P(None, None, None, 'gz', 'xy'), may hold values from -0.59765625 to 0.59765625
- block_inv: bfloat16 [12, 12, 8, 16, 512], P(None, None, 'gz', 'xy'), may hold values from -0.125 to 0.405
- press_weight: bfloat16 [12, 8, 16, 512], P(None, 'gz', 'xy'), may hold values from 0.099609375 to 1
- press_diag: bfloat16 [8, 16, 512], P('gz', 'xy'), may hold values from 6.5 to 9
- press_off: bfloat16 [6, 8, 16, 512], P(None, 'gz', 'xy'), may hold values from -1 to -0.19921875
- well_index: float32 [8, 16, 512], P('gz', 'xy'), may hold values from 0.5 to 5
- well_columns: int32 [64], replicated, may hold values from 0 to 8191
- agg_map: int32 [8, 16, 512], P('gz', 'xy'), may hold values from 0 to 7
- level1_op: bfloat16 [8, 8, 8, 16, 4], P(None, None, 'gz', 'xy'), may hold values from -1.65 to 5.05
- coarsest_inv: bfloat16 [8, 16, 8, 16], P('gz', 'xy'), may hold values from -0.13479223 to 0.31156893
Outputs:
- solution: float32 [12, 8, 16, 512], P(None, 'gz', 'xy')
- residual: float32 [12, 8, 16, 512], P(None, 'gz', 'xy')
- hessenberg: float32 [3, 2], replicated
The draws below stay inside these ranges and needn't reach their ends.
Inputs may be any that keep to these rules, and one draw needn't show every extreme that they name: `well_columns`: flat areal index x * 512 + y of each vertical well, which is perforated in every layer; a column may hold several wells. `agg_map`: an aggregate may be empty.
All inputs are finite; a program needn't handle non-finite values.
Results may differ from the reference program's by a relative error of at most 0.0018.
Values may be sent and summed in bfloat16 or wider, within the bound.
A program may use at most 64 MiB of HBM per device.

```python
import math
import jax
import jax.numpy as jnp
from jax import lax

NC = 12
NY = 512
BLK = 128
AGG = 8
NW = 64
ITERS = 2
NZ = 8
NX = 16
NB = 4


def diagonal_blocks(key, count, trailing, low, high, noise_scale):
    noise_key, middle_key = jax.random.split(key)
    shape = (count, count) + trailing
    noise = noise_scale * jnp.clip(jax.random.normal(noise_key, shape, jnp.float32), -4.0, 4.0)
    middle = jax.random.uniform(middle_key, (count,) + trailing, jnp.float32, low, high)
    identity = jnp.eye(count, dtype=jnp.float32).reshape((count, count) + (1,) * len(trailing))
    return noise * (1.0 - identity) + identity * middle[None]


def draw_jac_diag(key, part):
    blocks = diagonal_blocks(key, NC, (NZ, NX, NY), 3.0, 6.0, 0.3)
    return blocks.astype(jnp.bfloat16)


def draw_block_inv(key, part):
    blocks = diagonal_blocks(key, NC, (NZ, NX, NY), 0.17, 0.33, 0.03)
    return blocks.astype(jnp.bfloat16)


def draw_level1_op(key, part):
    blocks = diagonal_blocks(key, AGG, (NZ, NX, NB), 2.0, 4.0, 0.4)
    return blocks.astype(jnp.bfloat16)


def draw_coarsest_inv(key, part):
    order = NZ * NX
    scale = NY ** (-0.5)
    spread = scale * order ** (-0.5)
    blocks = diagonal_blocks(key, order, (), 3.0 * scale, 6.0 * scale, 3.6 * spread)
    return blocks.reshape(NZ, NX, NZ, NX).astype(jnp.bfloat16)


def touch_ends(values, rng, least, largest):
    place = [jax.random.randint(jax.random.fold_in(rng, axis), (), 0, length) for axis, length in enumerate(values.shape)]
    longest = values.shape.index(max(values.shape))
    beside = place[:longest] + [(place[longest] + 1) % values.shape[longest]] + place[longest + 1:]
    return values.at[tuple(place)].set(least).at[tuple(beside)].set(largest)


def block_scale(own_key, extent, pieces, smallest, largest):
    loudness, own = 1.0, jax.random.fold_in(own_key, 6)
    for axis_at, parts in pieces:
        draws = jnp.exp(jax.random.uniform(jax.random.fold_in(own, axis_at), (parts,), jnp.float32, smallest / len(pieces), largest / len(pieces)))
        loudness = loudness * jnp.repeat(draws, extent[axis_at] // parts).reshape([-1 if axis == axis_at else 1 for axis in range(len(extent))])
    return loudness


def scatter_about(rng, shape, deviation, most, shards=(), kind=jnp.bfloat16):
    values = jax.random.normal(rng, shape, jnp.float32) * deviation
    if len(shards) > 0:
        values = block_scale(rng, shape, shards, -0.22, 0.18) * values
    return jnp.clip(values, min=-most, max=most).astype(kind)


def setup_inputs(seed: int = 0) -> dict:
    arg_keys = jax.random.split(jax.random.key(seed), 13)
    right_side = scatter_about(arg_keys[0], (NC, NZ, NX, NY), 4.0, 24.0, ((1, 4), (2, 8)), jnp.float32)
    jac_diag = draw_jac_diag(jax.random.fold_in(arg_keys[12], 71), 0)
    jac_off = scatter_about(arg_keys[2], (6, NC, NC, NZ, NX, NY), 0.1, 0.59765625, ((3, 4), (4, 8)))
    block_inv = draw_block_inv(jax.random.fold_in(arg_keys[12], 71), 0)
    press_weight = jnp.clip(0.099609375 + 0.9003906 * jax.random.uniform(arg_keys[4], (NC, NZ, NX, NY), jnp.float32) ** block_scale(arg_keys[4], (NC, NZ, NX, NY), ((1, 4), (2, 8)), -0.2, 0.2), 0.099609375, 1.0).astype(jnp.bfloat16)
    press_diag = jnp.clip(6.5 + 2.5 * jax.random.uniform(arg_keys[5], (NZ, NX, NY), jnp.float32) ** block_scale(arg_keys[5], (NZ, NX, NY), ((0, 4), (1, 8)), -0.2, 0.2), 6.5, 9.0).astype(jnp.bfloat16)
    press_off = jnp.clip(-1.0 + 0.80078125 * jax.random.uniform(arg_keys[6], (6, NZ, NX, NY), jnp.float32) ** block_scale(arg_keys[6], (6, NZ, NX, NY), ((1, 4), (2, 8)), -0.2, 0.2), -1.0, -0.19921875).astype(jnp.bfloat16)
    well_index = jnp.clip(jnp.exp(math.log(5.0) - 2.3025851 * jax.random.uniform(arg_keys[7], (NZ, NX, NY), jnp.float32) ** block_scale(arg_keys[7], (NZ, NX, NY), ((0, 4), (1, 8)), -0.2, 0.2)), 0.5, 5.0)
    well_columns = touch_ends(jax.random.randint(arg_keys[8], (NW,), 0, NX * NY), jax.random.fold_in(arg_keys[8], 1), 0, (NX * NY) - 1).astype(jnp.int32)
    agg_map = touch_ends(jax.random.randint(arg_keys[9], (NZ, NX, NY), 0, AGG), jax.random.fold_in(arg_keys[9], 1), 0, AGG - 1).astype(jnp.int32)
    level1_op = draw_level1_op(jax.random.fold_in(arg_keys[12], 71), 0)
    coarsest_inv = draw_coarsest_inv(jax.random.fold_in(arg_keys[12], 71), 0)
    return dict(right_side=right_side, jac_diag=jac_diag, jac_off=jac_off, block_inv=block_inv, press_weight=press_weight, press_diag=press_diag, press_off=press_off, well_index=well_index, well_columns=well_columns, agg_map=agg_map, level1_op=level1_op, coarsest_inv=coarsest_inv)


EPSILON = 1e-06

def neighbours(padded):
    return jnp.stack([padded[..., :-2, 1:-1, 1:-1], padded[..., 2:, 1:-1, 1:-1], padded[..., 1:-1, :-2, 1:-1], padded[..., 1:-1, 2:, 1:-1], padded[..., 1:-1, 1:-1, :-2], padded[..., 1:-1, 1:-1, 2:]])

def layer_apply(field, centre_blocks, side_blocks):
    padded = jnp.pad(field, ((0, 0), (1, 1), (1, 1), (1, 1)))

    def layer(level):
        slab = lax.dynamic_slice_in_dim(padded, level, 3, 1)
        near = neighbours(slab)[:, :, 0]
        centre = slab[:, 1, 1:-1, 1:-1]
        centre_layer = lax.dynamic_index_in_dim(centre_blocks, level, 2, keepdims=False).astype(jnp.float32)
        side_layer = lax.dynamic_index_in_dim(side_blocks, level, 3, keepdims=False).astype(jnp.float32)
        return lax.optimization_barrier(jnp.sum(centre_layer * centre[None], axis=1)) + lax.optimization_barrier(jnp.sum(side_layer * near[:, None], axis=(0, 2)))
    return jnp.moveaxis(lax.map(layer, jnp.arange(NZ, dtype=jnp.int32)), 0, 1)

def block_apply(blocks, field):

    def layer(level):
        block_layer = lax.dynamic_index_in_dim(blocks, level, 2, keepdims=False).astype(jnp.float32)
        field_layer = lax.dynamic_index_in_dim(field, level, 1, keepdims=False)
        return lax.optimization_barrier(jnp.sum(block_layer * field_layer[None], axis=1))
    return jnp.moveaxis(lax.map(layer, jnp.arange(NZ, dtype=jnp.int32)), 0, 1)

def least_squares(hessen, beta):
    upper = [list(line) for line in hessen]
    target = [beta] + [jnp.zeros((), jnp.float32) for line in range(ITERS)]
    rotations = []
    for column in range(ITERS):
        for row, (cosine, sine) in enumerate(rotations):
            first, second = (upper[row][column], upper[row + 1][column])
            upper[row][column] = cosine * first + sine * second
            upper[row + 1][column] = cosine * second - sine * first
        first, second = (upper[column][column], upper[column + 1][column])
        radius = jnp.sqrt(first * first + second * second)
        cosine, sine = (first / radius, second / radius)
        upper[column][column] = radius
        leading = target[column]
        target[column] = cosine * leading
        target[column + 1] = -sine * leading
        rotations.append((cosine, sine))
    weights = [None] * ITERS
    for column in reversed(range(ITERS)):
        total = target[column]
        for later in range(column + 1, ITERS):
            total = total - upper[column][later] * weights[later]
        weights[column] = total / upper[column][column]
    return weights

def reference(right_side, jac_diag, jac_off, block_inv, press_weight, press_diag, press_off, well_index, well_columns, agg_map, level1_op, coarsest_inv):
    columns = jnp.arange(NX * NY, dtype=jnp.int32)
    well_mask = (well_columns[:, None] == columns[None, :]).astype(jnp.float32)
    wells_here = lax.optimization_barrier(jnp.sum(well_mask, axis=0)).reshape(NX, NY)
    well_weight = jnp.dot(well_mask, lax.optimization_barrier(jnp.sum(well_index, axis=0)).reshape(-1), precision=lax.Precision.HIGHEST)

    def well_term(pressure):
        totals = jnp.dot(well_mask, lax.optimization_barrier(jnp.sum(well_index * pressure, axis=0)).reshape(-1), precision=lax.Precision.HIGHEST)
        spread = jnp.dot(totals / well_weight, well_mask, precision=lax.Precision.HIGHEST).reshape(NX, NY)
        return well_index * (wells_here * pressure - spread)

    def apply_fine(field):
        result = layer_apply(field, jac_diag, jac_off)
        return result.at[0].add(well_term(field[0]))

    def apply_column(pressure):
        result = layer_apply(pressure[None], jac_diag[:, 0:1], jac_off[:, :, 0:1])
        return result.at[0].add(well_term(pressure))
    diag_pressure = press_diag.astype(jnp.float32)

    def apply_pressure(field):
        near = neighbours(jnp.pad(field, 1))
        return diag_pressure * field + lax.optimization_barrier(jnp.sum(press_off.astype(jnp.float32) * near, axis=0))
    one_hot = (agg_map[None] == jnp.arange(AGG, dtype=jnp.int32)[:, None, None, None]).astype(jnp.float32)
    coarse_op = level1_op.astype(jnp.float32)
    coarse_diag = jnp.stack([coarse_op[index, index] for index in range(AGG)])

    def precondition(vector):
        pressure_rhs = lax.optimization_barrier(jnp.sum(press_weight.astype(jnp.float32) * vector, axis=0))
        first_guess = pressure_rhs / diag_pressure
        fine_rest = pressure_rhs - apply_pressure(first_guess)
        coarse_rhs = lax.optimization_barrier(jnp.sum((one_hot * fine_rest[None]).reshape(AGG, NZ, NX, NB, BLK), axis=-1))
        coarse_guess = coarse_rhs / coarse_diag
        coarse_rest = coarse_rhs - lax.optimization_barrier(jnp.sum(coarse_op * coarse_guess[None], axis=1))
        coarsest_rhs = lax.optimization_barrier(jnp.sum(coarse_rest, axis=(0, 3))).astype(jnp.bfloat16)
        coarsest = jnp.dot(coarsest_inv.reshape(NZ * NX, NZ * NX), coarsest_rhs.reshape(-1), preferred_element_type=jnp.float32).reshape(NZ, NX)
        coarse_value = coarse_guess + coarsest[None, :, :, None]
        smooth_guess = first_guess + lax.optimization_barrier(jnp.sum(one_hot * jnp.repeat(coarse_value, BLK, axis=-1), axis=0))
        pressure = smooth_guess + (pressure_rhs - apply_pressure(smooth_guess)) / diag_pressure
        remainder = vector - apply_column(pressure)
        correction = block_apply(block_inv, remainder)
        return correction.at[0].add(pressure)
    beta = jnp.sqrt(jnp.sum(right_side * right_side) + EPSILON)
    basis = [right_side / beta]
    directions = []
    hessen = [[jnp.zeros((), jnp.float32) for column in range(ITERS)] for row in range(ITERS + 1)]
    for step in range(ITERS):
        direction = precondition(basis[step])
        image = apply_fine(direction)
        directions.append(direction)
        for row in range(step + 1):
            hessen[row][step] = jnp.sum(image * basis[row])
        rest = image
        for row in range(step + 1):
            rest = rest - hessen[row][step] * basis[row]
        height = jnp.sqrt(jnp.sum(rest * rest) + EPSILON)
        hessen[step + 1][step] = height
        if step + 1 < ITERS:
            basis.append(rest / height)
    weights = least_squares(hessen, beta)
    solution = weights[0] * directions[0]
    for step in range(1, ITERS):
        solution = solution + weights[step] * directions[step]
    residual = right_side - apply_fine(solution)
    hessenberg = jnp.stack([jnp.stack(line) for line in hessen])
    return (solution, residual, hessenberg)
```

```python
import functools

import jax
import jax.numpy as jnp
from jax import lax
from jax.experimental import pallas as pl
from jax.experimental.pallas import tpu as pltpu
from jax.sharding import PartitionSpec as P

ITERS = 2
EPSILON = 1e-06
LANES = 128
TINY = 1e-30
F32 = jnp.float32
MESH = pl.DeviceIdType.MESH
ROUNDS = 6


def kernel(
    depth, width, length, layer_devices, areal_devices, halves,
    rs, pw, pd, po, wi, wc, agg, lvl, inv, jd_hbm, jo_hbm, bi_hbm,
    sol, res, hess,
    jd, jo, bi, basis, dirs, imgs, near, rem, cvec,
    fld, pkx, hz, hx, pkx12, hz12, hx12,
    invs, invh, rows_src, gath, co_src, co_gath, col_src, peer,
    hbm_sem, halo_send, halo_recv, big_send, big_recv, inv_send, inv_recv,
    row_send, row_recv, co_send, co_recv, peer_send, peer_recv,
):
    comps = rs.shape[0]
    strips = length // LANES
    plane = strips * width
    total = depth * plane
    count = layer_devices * areal_devices
    points = depth * width
    co_rows = invs.shape[0] // points
    aggregates = halves
    g = lax.axis_index("gz")
    e = lax.axis_index("xy")
    me = g * areal_devices + e

    def at(index):
        return {"gz": index // areal_devices, "xy": index % areal_devices}

    barrier = pltpu.get_barrier_semaphore()

    def greet(step, carry):
        pl.semaphore_signal(
            barrier, inc=1, device_id=at((me + step) % count), device_id_type=MESH
        )
        return carry

    lax.fori_loop(1, count, greet, 0)

    loads = [
        pltpu.make_async_copy(jd_hbm, jd, hbm_sem.at[0]),
        pltpu.make_async_copy(bi_hbm, bi, hbm_sem.at[1]),
        pltpu.make_async_copy(jo_hbm, jo, hbm_sem.at[2]),
    ]
    for load in loads:
        load.start()

    row_at = lax.broadcasted_iota(jnp.int32, (plane, LANES), 0)
    lane_at = lax.broadcasted_iota(jnp.int32, (plane, LANES), 1)
    x_at = row_at % width
    strip_at = row_at // width
    lane_row = lax.broadcasted_iota(jnp.int32, (1, LANES), 1)

    def roll(a, shift, axis):
        size = a.shape[axis]
        shift = shift % size
        return a if shift == 0 else pltpu.roll(a, shift, axis)

    def planes(a):
        return a.reshape(-1, plane, LANES)

    def pack(a, edge):
        p = planes(a).reshape(-1, depth, plane, LANES)
        groups = -(-depth // width)
        out = []
        for group in range(groups):
            acc = jnp.zeros((p.shape[0], plane, LANES), F32)
            for s in range(group * width, min(depth, (group + 1) * width)):
                moved = roll(p[:, s], s % width - edge, 1)
                acc = jnp.where((x_at == s % width)[None], moved, acc)
            out.append(acc)
        return out[0] if groups == 1 else jnp.concatenate(out, axis=1)

    def unpack(b, target):
        parts = []
        for s in range(depth):
            group = s // width
            piece = b[:, group * plane:(group + 1) * plane]
            parts.append(roll(piece, target - s % width, 1))
        return jnp.concatenate(parts, axis=1)

    def tile_rows(mask):
        return jnp.concatenate([mask] * depth, axis=0)[None]

    x_all = tile_rows(x_at)
    def shift_zl(f, h):
        return jnp.concatenate([h, f[:, :-plane]], axis=1) if depth > 1 else h

    def shift_zh(f, h):
        return jnp.concatenate([f[:, plane:], h], axis=1) if depth > 1 else h

    def shift_xl(f, h):
        own = roll(planes(f), 1, 1).reshape(f.shape)
        return jnp.where(x_all == 0, h, own)

    def shift_xh(f, h):
        own = roll(planes(f), -1, 1).reshape(f.shape)
        return jnp.where(x_all == width - 1, h, own)

    def shift_yl(f):
        p = planes(f)
        t = roll(p, 1, 2)
        u = roll(t, width, 1)
        first = (lane_at == 0)[None]
        edge = (strip_at == 0)[None]
        return jnp.where(first, jnp.where(edge, 0.0, u), t).reshape(f.shape)

    def shift_yh(f):
        p = planes(f)
        t = roll(p, -1, 2)
        u = roll(t, -width, 1)
        last = (lane_at == LANES - 1)[None]
        edge = (strip_at == strips - 1)[None]
        return jnp.where(last, jnp.where(edge, 0.0, u), t).reshape(f.shape)

    to = [
        (g < layer_devices - 1, g > 0, {"gz": g + 1, "xy": e}),
        (g > 0, g < layer_devices - 1, {"gz": g - 1, "xy": e}),
        (e < areal_devices - 1, e > 0, {"gz": g, "xy": e + 1}),
        (e > 0, e < areal_devices - 1, {"gz": g, "xy": e - 1}),
    ]

    @pl.when(g == 0)
    def _():
        hz[:, 0] = jnp.zeros(hz.shape[:1] + hz.shape[2:], F32)
        hz12[:, 0] = jnp.zeros(hz12.shape[:1] + hz12.shape[2:], F32)
        invh[0] = jnp.zeros(invh.shape[1:], F32)

    @pl.when(g == layer_devices - 1)
    def _():
        hz[:, 1] = jnp.zeros(hz.shape[:1] + hz.shape[2:], F32)
        hz12[:, 1] = jnp.zeros(hz12.shape[:1] + hz12.shape[2:], F32)
        invh[1] = jnp.zeros(invh.shape[1:], F32)

    @pl.when(e == 0)
    def _():
        hx[:, 0] = jnp.zeros(hx.shape[:1] + hx.shape[2:], F32)
        hx12[:, 0] = jnp.zeros(hx12.shape[:1] + hx12.shape[2:], F32)
        invh[2] = jnp.zeros(invh.shape[1:], F32)

    @pl.when(e == areal_devices - 1)
    def _():
        hx[:, 1] = jnp.zeros(hx.shape[:1] + hx.shape[2:], F32)
        hx12[:, 1] = jnp.zeros(hx12.shape[:1] + hx12.shape[2:], F32)
        invh[3] = jnp.zeros(invh.shape[1:], F32)

    finals = []

    def halo_copies(r):
        srcs = [
            fld.at[r, pl.ds(total - plane, plane)],
            fld.at[r, pl.ds(0, plane)],
            pkx.at[r, 0],
            pkx.at[r, 1],
        ]
        dsts = [hz.at[r, 0], hz.at[r, 1], hx.at[r, 0], hx.at[r, 1]]
        return [
            pltpu.make_async_remote_copy(
                src_ref=srcs[d], dst_ref=dsts[d], send_sem=halo_send.at[r, d],
                recv_sem=halo_recv.at[r, d], device_id=to[d][2], device_id_type=MESH,
            )
            for d in range(4)
        ]

    def big_copies(t):
        srcs = [
            dirs.at[t, :, pl.ds(total - plane, plane)],
            dirs.at[t, :, pl.ds(0, plane)],
            pkx12.at[t, 0],
            pkx12.at[t, 1],
        ]
        dsts = [hz12.at[t, 0], hz12.at[t, 1], hx12.at[t, 0], hx12.at[t, 1]]
        return [
            pltpu.make_async_remote_copy(
                src_ref=srcs[d], dst_ref=dsts[d], send_sem=big_send.at[t, d],
                recv_sem=big_recv.at[t, d], device_id=to[d][2], device_id_type=MESH,
            )
            for d in range(4)
        ]

    def inv_copies():
        return [
            pltpu.make_async_remote_copy(
                src_ref=invs, dst_ref=invh.at[d], send_sem=inv_send.at[d],
                recv_sem=inv_recv.at[d], device_id=to[d][2], device_id_type=MESH,
            )
            for d in range(4)
        ]

    def start_all(copies):
        for d in range(4):
            pl.when(to[d][0])(copies[d].start)
            finals.append((to[d][0], copies[d].wait_send))

    def arrive(copies):
        for d in range(4):
            pl.when(to[d][1])(copies[d].wait_recv)

    def halo_start(r, f):
        fld[r] = f
        pkx[r, 0] = pack(f[None], width - 1)[0]
        pkx[r, 1] = pack(f[None], 0)[0]
        copies = halo_copies(r)
        start_all(copies)
        return copies

    def halo_read(r):
        return (
            hz[r, 0][None], hz[r, 1][None],
            unpack(hx[r, 0][None], 0), unpack(hx[r, 1][None], width - 1),
        )

    def send_all(src, dst, size, send, recv):
        def one(step, carry):
            pltpu.make_async_remote_copy(
                src_ref=src, dst_ref=dst.at[pl.ds(me * size, size)], send_sem=send,
                recv_sem=recv, device_id=at((me + step) % count), device_id_type=MESH,
            ).start()
            return carry

        lax.fori_loop(1, count, one, 0)
        whole = dst.at[pl.ds(0, (count - 1) * size)]
        finals.append((None, pltpu.make_async_copy(whole, whole, send).wait))
        return pltpu.make_async_copy(whole, whole, recv).wait

    def rows_start(r, values):
        row = jnp.zeros((1, LANES), F32)
        for q, value in enumerate(values):
            row = jnp.where(lane_row == q, value, row)
        rows_src[r] = row
        gath[r, pl.ds(me, 1)] = row
        return send_all(rows_src.at[r], gath.at[r], 1, row_send.at[r], row_recv.at[r])

    def rows_read(r, n):
        got = gath[r]
        lanes = lax.broadcasted_iota(jnp.int32, got.shape, 1)
        return [
            jnp.sum(jnp.where(lanes == q, got, 0.0), axis=1, keepdims=True) for q in range(n)
        ]

    def peers_start(r, value):
        col_src[r] = value
        peer[r, g] = value
        for step in range(1, layer_devices):
            pltpu.make_async_remote_copy(
                src_ref=col_src.at[r], dst_ref=peer.at[r, g], send_sem=peer_send.at[r],
                recv_sem=peer_recv.at[r],
                device_id={"gz": (g + step) % layer_devices, "xy": e}, device_id_type=MESH,
            ).start()
        whole = peer.at[r, pl.ds(0, layer_devices - 1)]
        finals.append((None, pltpu.make_async_copy(whole, whole, peer_send.at[r]).wait))
        return pltpu.make_async_copy(whole, whole, peer_recv.at[r]).wait

    def over_planes(f):
        acc = f[0:plane]
        for z in range(1, depth):
            acc = acc + f[z * plane:(z + 1) * plane]
        return acc

    def scalar(a):
        a = jnp.sum(a, axis=0) if a.ndim == 3 else a
        return jnp.sum(jnp.sum(a, axis=0, keepdims=True), axis=1, keepdims=True)

    def ssum(a):
        return jnp.sum(a, axis=0, keepdims=True)

    diag = pd[...].astype(F32)
    sides = po[...].astype(F32)
    rs_all = rs[...]
    raw_rhs = jnp.sum(pw[...].astype(F32) * rs_all, axis=0)
    raw_guess = raw_rhs / diag
    norm_here = scalar(rs_all * rs_all)
    index = wi[...]
    weight_here = over_planes(index)
    invs[...] = inv[...].astype(F32)
    column = (e * width + x_at) * length + strip_at * LANES + lane_at

    pl.semaphore_wait(barrier, count - 1)
    norm_wait = rows_start(0, [norm_here])
    halo_a = halo_start(0, raw_guess)
    inv_all = inv_copies()
    start_all(inv_all)
    weight_wait = peers_start(0, weight_here)

    def tally(w, acc):
        return acc + jnp.where(column == wc[w], 1.0, 0.0)

    wells = lax.fori_loop(0, wc.shape[0], tally, jnp.zeros((plane, LANES), F32))
    wells = jnp.concatenate([wells] * depth, axis=0)
    well_factor = index * wells
    aggs = agg[...]

    def apply_pressure(f, halos):
        f3 = f[None]
        nears = [
            shift_zl(f3, halos[0]), shift_zh(f3, halos[1]),
            shift_xl(f3, halos[2]), shift_xh(f3, halos[3]),
            shift_yl(f3), shift_yh(f3),
        ]
        out = diag * f
        for k in range(6):
            out = out + sides[k] * nears[k][0]
        return out

    def well_start(r, q):
        return peers_start(r, over_planes(index * q))

    norm_wait()
    beta = jnp.sqrt(ssum(rows_read(0, 1)[0]) + EPSILON)
    arrive(halo_a)
    guess_halos = [h / beta for h in halo_read(0)]
    arrive(inv_all)
    basis[0] = rs_all / beta
    rhs = raw_rhs / beta
    guess = raw_guess / beta

    col_weight = None
    hessen = [[jnp.zeros((1, 1), F32) for _ in range(ITERS)] for _ in range(ITERS + 1)]
    lane_all = lax.broadcasted_iota(jnp.int32, (total, LANES), 1)
    flat_at = (
        lax.broadcasted_iota(jnp.int32, (co_rows, LANES), 0) * LANES
        + lax.broadcasted_iota(jnp.int32, (co_rows, LANES), 1)
    )
    gram = None
    for t in range(ITERS):
        v = basis.at[t]
        rest = rhs - apply_pressure(guess, guess_halos)
        colsum = lvl[0]
        codiag = lvl[1]
        coarse = jnp.zeros((total, LANES), F32)
        for a in range(aggregates):
            part = jnp.sum(jnp.where(aggs == a, rest, 0.0), axis=1, keepdims=True)
            coarse = jnp.where(lane_all == a, part, coarse)
        coarse_guess = coarse / codiag
        coarse_rest = jnp.sum(coarse - colsum * coarse_guess, axis=1, keepdims=True)
        message = jnp.zeros((co_rows, LANES), F32)
        for z in range(depth):
            part = coarse_rest[z * plane:(z + 1) * plane]
            for x in range(width):
                value = jnp.sum(
                    jnp.where(x_at[:, 0:1] == x, part, 0.0), axis=0, keepdims=True
                )
                spot = (g * depth + z) * (areal_devices * width) + e * width + x
                message = jnp.where(flat_at == spot, value, message)
        message = message.astype(jnp.bfloat16).astype(F32)
        co_src[t] = message
        co_gath[t, pl.ds(me * co_rows, co_rows)] = message
        co_wait = send_all(co_src.at[t], co_gath.at[t], co_rows, co_send.at[t], co_recv.at[t])
        picked = guess
        for a in range(aggregates):
            picked = jnp.where(aggs == a, guess + coarse_guess[:, a:a + 1], picked)
        halo_b = halo_start(1 + 3 * t, picked)
        if t == 0:
            weight_wait()
            col_weight = jnp.sum(peer[0], axis=0)
        b0 = basis[0]
        if t == 0:
            g00 = scalar(b0 * b0)
        else:
            b1 = basis[1]
            g00, g01 = gram[0], scalar(b0 * b1)
            tilt = jnp.where(g00 > TINY, g01 / g00, 0.0)
            perp = b1 - tilt * b0
            cvec[...] = perp
            cc = scalar(perp * perp)
        gram = (g00,)
        co_wait()
        ordered = jnp.sum(co_gath[t].reshape(count, co_rows, LANES), axis=0)

        def coarsest_of(mat):
            prod = mat.reshape(points, co_rows, LANES) * ordered[None]
            return jnp.sum(jnp.sum(prod, axis=1), axis=1, keepdims=True)

        def layer_of(values, z):
            acc = jnp.zeros((plane, LANES), F32)
            for x in range(width):
                at_point = z * width + x
                acc = jnp.where(x_at == x, values[at_point:at_point + 1], acc)
            return acc

        def spread_of(values):
            return jnp.concatenate([layer_of(values, z) for z in range(depth)], axis=0)

        def edge_of(values, x):
            parts = [
                jnp.broadcast_to(
                    values[z * width + x:z * width + x + 1], (plane, LANES)
                )
                for z in range(depth)
            ]
            return jnp.concatenate(parts, axis=0)

        smooth = picked + spread_of(coarsest_of(invs[...]))
        halo_extra = [
            layer_of(coarsest_of(invh[0]), depth - 1),
            layer_of(coarsest_of(invh[1]), 0),
            edge_of(coarsest_of(invh[2]), width - 1),
            edge_of(coarsest_of(invh[3]), 0),
        ]
        arrive(halo_b)
        got = halo_read(1 + 3 * t)
        smooth_halos = [got[d] + halo_extra[d][None] for d in range(4)]
        pressure = smooth + (rhs - apply_pressure(smooth, smooth_halos)) / diag
        halo_d = halo_start(2 + 3 * t, pressure)
        well_wait = well_start(1 + 2 * t, pressure)
        if t == 0:
            for load in loads:
                load.wait()
        p3 = pressure[None]
        acc = v[...] - jd[:, 0].astype(F32) * p3
        acc = acc - jo[4, :, 0].astype(F32) * shift_yl(p3)
        acc = acc - jo[5, :, 0].astype(F32) * shift_yh(p3)
        arrive(halo_d)
        got = halo_read(2 + 3 * t)
        acc = acc - jo[0, :, 0].astype(F32) * shift_zl(p3, got[0])
        acc = acc - jo[1, :, 0].astype(F32) * shift_zh(p3, got[1])
        acc = acc - jo[2, :, 0].astype(F32) * shift_xl(p3, got[2])
        acc = acc - jo[3, :, 0].astype(F32) * shift_xh(p3, got[3])
        rem[...] = acc

        def well_term(r, q):
            level = jnp.sum(peer[r], axis=0) / col_weight
            return well_factor * (q - jnp.concatenate([level] * depth, axis=0))

        well_wait()
        rem[0] = rem[0] - well_term(1 + 2 * t, pressure)

        def correct(i, carry):
            dirs[t, i] = jnp.sum(bi[i].astype(F32) * rem[...], axis=0)
            return carry

        lax.fori_loop(0, comps, correct, 0)
        head = dirs[t, 0] + pressure
        dirs[t, 0] = head
        d_all = dirs[t]
        pkx12[t, 0] = pack(d_all, width - 1)
        pkx12[t, 1] = pack(d_all, 0)
        big = big_copies(t)
        start_all(big)
        well_wait = well_start(2 + 2 * t, head)
        near[4] = shift_yl(d_all)
        near[5] = shift_yh(d_all)

        def inner(i, carry):
            out = jnp.sum(jd[i].astype(F32) * dirs[t], axis=0)
            for k in (4, 5):
                out = out + jnp.sum(jo[k, i].astype(F32) * near[k], axis=0)
            imgs[t, i] = out
            return carry

        lax.fori_loop(0, comps, inner, 0)
        arrive(big)
        d_all = dirs[t]
        near[0] = shift_zl(d_all, hz12[t, 0])
        near[1] = shift_zh(d_all, hz12[t, 1])
        near[2] = shift_xl(d_all, unpack(hx12[t, 0], 0))
        near[3] = shift_xh(d_all, unpack(hx12[t, 1], width - 1))

        def outer(i, carry):
            out = imgs[t, i]
            for k in range(4):
                out = out + jnp.sum(jo[k, i].astype(F32) * near[k], axis=0)
            imgs[t, i] = out
            return carry

        lax.fori_loop(0, comps, outer, 0)
        well_wait()
        imgs[t, 0] = imgs[t, 0] + well_term(2 + 2 * t, head)
        image = imgs[t]
        b0 = basis[0]
        p0 = scalar(image * b0)
        a0 = jnp.where(g00 > TINY, p0 / g00, 0.0)
        if t == 0:
            left = image - a0 * b0
            rr = scalar(left * left)
            row_wait = rows_start(1, [p0, g00, a0, rr])
            image_guess = jnp.sum(pw[...].astype(F32) * image, axis=0) / diag
            halo_f = halo_start(3, image_guess)
            row_wait()
            q0, gg, aa, ll = rows_read(1, 4)
            h00 = ssum(q0)
            height = jnp.sqrt(ssum(ll + (aa - h00) * (aa - h00) * gg) + EPSILON)
            hessen[0][0] = h00
            hessen[1][0] = height
            next_basis = (image - h00 * b0) / height
            basis[1] = next_basis
            rhs = jnp.sum(pw[...].astype(F32) * next_basis, axis=0)
            guess = rhs / diag
            arrive(halo_f)
            got = halo_read(3)
            guess_halos = [(got[d] - h00 * guess_halos[d]) / height for d in range(4)]
        else:
            perp = cvec[...]
            p1 = scalar(image * basis[1])
            a1 = jnp.where(cc > TINY, scalar(image * perp) / cc, 0.0)
            left = image - a0 * b0 - a1 * perp
            rr = scalar(left * left)
            row_wait = rows_start(2, [p0, p1, g00, tilt, a0, cc, a1, rr])
            row_wait()
            q0, q1, gg, ee, aa0, cc1, aa1, ll = rows_read(2, 8)
            h0 = ssum(q0)
            h1 = ssum(q1)
            d0 = aa0 - h0 - ee * h1
            d1 = aa1 - h1
            hessen[0][1] = h0
            hessen[1][1] = h1
            hessen[2][1] = jnp.sqrt(ssum(ll + d0 * d0 * gg + d1 * d1 * cc1) + EPSILON)

    weights = least_squares(hessen, beta)
    sol[...] = weights[0] * dirs[0] + weights[1] * dirs[1]
    res[...] = rs[...] - (weights[0] * imgs[0] + weights[1] * imgs[1])
    hr = lax.broadcasted_iota(jnp.int32, hess.shape, 0)
    hc = lax.broadcasted_iota(jnp.int32, hess.shape, 1)
    table = jnp.zeros(hess.shape, F32)
    for i in range(ITERS + 1):
        for j in range(ITERS):
            table = jnp.where((hr == i) & (hc == j), hessen[i][j], table)
    hess[...] = table
    for condition, wait in finals:
        if condition is None:
            wait()
        else:
            pl.when(condition)(wait)


def least_squares(hessen, beta):
    upper = [list(line) for line in hessen]
    target = [beta] + [jnp.zeros((1, 1), F32) for line in range(ITERS)]
    rotations = []
    for column in range(ITERS):
        for row, (cosine, sine) in enumerate(rotations):
            first, second = (upper[row][column], upper[row + 1][column])
            upper[row][column] = cosine * first + sine * second
            upper[row + 1][column] = cosine * second - sine * first
        first, second = (upper[column][column], upper[column + 1][column])
        radius = jnp.sqrt(first * first + second * second)
        cosine, sine = (first / radius, second / radius)
        upper[column][column] = radius
        leading = target[column]
        target[column] = cosine * leading
        target[column + 1] = -sine * leading
        rotations.append((cosine, sine))
    weights = [None] * ITERS
    for column in reversed(range(ITERS)):
        total = target[column]
        for later in range(column + 1, ITERS):
            total = total - upper[column][later] * weights[later]
        weights[column] = total / upper[column][column]
    return weights


def to_rows(a):
    depth, width, length = a.shape[-3:]
    lead = a.shape[:-3]
    strips = length // LANES
    a = a.reshape(lead + (depth, width, strips, LANES))
    return jnp.swapaxes(a, -3, -2).reshape(lead + (depth * strips * width, LANES))


def from_rows(a, depth, width, length):
    lead = a.shape[:-2]
    strips = length // LANES
    a = a.reshape(lead + (depth, strips, width, LANES))
    return jnp.swapaxes(a, -3, -2).reshape(lead + (depth, width, length))


def on_device(
    right_side, jac_diag, jac_off, block_inv, press_weight, press_diag, press_off,
    well_index, well_columns, agg_map, level1_op, coarsest_inv,
):
    comps, depth, width, length = right_side.shape
    aggregates = level1_op.shape[0]
    blocks = level1_op.shape[4]
    layer_devices = lax.axis_size("gz")
    areal_devices = lax.axis_size("xy")
    count = layer_devices * areal_devices
    plane = (length // LANES) * width
    total = depth * plane
    points = depth * width
    op = level1_op.astype(F32)
    colsum = jnp.sum(op, axis=0)
    codiag = jnp.stack([op[a, a] for a in range(aggregates)])
    lane_pad = ((0, 0), (0, LANES - aggregates))
    order = (1, 3, 2, 0)
    colsum = colsum.transpose(order).reshape(total, aggregates)
    codiag = codiag.transpose(order).reshape(total, aggregates)
    lvl = jnp.stack(
        [jnp.pad(colsum, lane_pad), jnp.pad(codiag, lane_pad, constant_values=1.0)]
    )
    flat = coarsest_inv.shape[2] * coarsest_inv.shape[3]
    co_rows = flat // LANES
    inv = coarsest_inv.reshape(points * co_rows, LANES)

    vm = pl.BlockSpec(memory_space=pltpu.VMEM)
    sm = pl.BlockSpec(memory_space=pltpu.SMEM)
    anyspace = pl.BlockSpec(memory_space=pl.ANY)
    edge_rows = -(-depth // width) * plane
    v = pltpu.VMEM
    dma = pltpu.SemaphoreType.DMA
    scratch = [
        v((comps, comps, total, LANES), jnp.bfloat16),
        v((6, comps, comps, total, LANES), jnp.bfloat16),
        v((comps, comps, total, LANES), jnp.bfloat16),
        v((ITERS, comps, total, LANES), F32),
        v((ITERS, comps, total, LANES), F32),
        v((ITERS, comps, total, LANES), F32),
        v((6, comps, total, LANES), F32),
        v((comps, total, LANES), F32),
        v((comps, total, LANES), F32),
        v((ROUNDS, total, LANES), F32),
        v((ROUNDS, 2, edge_rows, LANES), F32),
        v((ROUNDS, 2, plane, LANES), F32),
        v((ROUNDS, 2, edge_rows, LANES), F32),
        v((ITERS, 2, comps, edge_rows, LANES), F32),
        v((ITERS, 2, comps, plane, LANES), F32),
        v((ITERS, 2, comps, edge_rows, LANES), F32),
        v((points * co_rows, LANES), F32),
        v((4, points * co_rows, LANES), F32),
        v((3, 1, LANES), F32),
        v((3, count, LANES), F32),
        v((ITERS, co_rows, LANES), F32),
        v((ITERS, count * co_rows, LANES), F32),
        v((5, plane, LANES), F32),
        v((5, layer_devices, plane, LANES), F32),
        dma((3,)),
        dma((ROUNDS, 4)), dma((ROUNDS, 4)),
        dma((ITERS, 4)), dma((ITERS, 4)),
        dma((4,)), dma((4,)),
        dma((3,)), dma((3,)),
        dma((ITERS,)), dma((ITERS,)),
        dma((5,)), dma((5,)),
    ]
    body = functools.partial(
        kernel, depth, width, length, layer_devices, areal_devices, aggregates
    )
    sol, res, hess = pl.pallas_call(
        body,
        out_shape=(
            jax.ShapeDtypeStruct((comps, total, LANES), F32),
            jax.ShapeDtypeStruct((comps, total, LANES), F32),
            jax.ShapeDtypeStruct((ITERS + 1, ITERS), F32),
        ),
        in_specs=[vm, vm, vm, vm, vm, sm, vm, vm, vm, anyspace, anyspace, anyspace],
        out_specs=(vm, vm, vm),
        scratch_shapes=scratch,
        compiler_params=pltpu.CompilerParams(
            collective_id=0, has_side_effects=True, vmem_limit_bytes=40 * 1024 * 1024
        ),
    )(
        to_rows(right_side), to_rows(press_weight), to_rows(press_diag), to_rows(press_off),
        to_rows(well_index), well_columns, to_rows(agg_map), lvl, inv,
        to_rows(jac_diag), to_rows(jac_off), to_rows(block_inv),
    )
    return (
        from_rows(sol, depth, width, length),
        from_rows(res, depth, width, length),
        hess,
    )


def solution(mesh):
    in_specs = (
        P(None, "gz", "xy", None),
        P(None, None, "gz", "xy", None),
        P(None, None, None, "gz", "xy", None),
        P(None, None, "gz", "xy", None),
        P(None, "gz", "xy", None),
        P("gz", "xy", None),
        P(None, "gz", "xy", None),
        P("gz", "xy", None),
        P(),
        P("gz", "xy", None),
        P(None, None, "gz", "xy", None),
        P("gz", "xy", None, None),
    )
    out_specs = (P(None, "gz", "xy", None), P(None, "gz", "xy", None), P())
    return jax.shard_map(
        on_device, mesh=mesh, in_specs=in_specs, out_specs=out_specs, check_vma=False
    )
```

```python
import functools

import jax
import jax.numpy as jnp
from jax import lax
from jax.experimental import pallas as pl
from jax.experimental.pallas import tpu as pltpu
from jax.sharding import PartitionSpec as P

ITERS = 2
EPSILON = 1e-06
LANES = 128
TINY = 1e-30
F32 = jnp.float32
MESH = pl.DeviceIdType.MESH
ROUNDS = 6


def kernel(
    depth, width, length, layer_devices, areal_devices, halves,
    rs_hbm, pw_hbm, pd_hbm, po_hbm, wi_hbm, wc_hbm, agg_hbm, lvl_hbm, inv_hbm,
    jd_hbm, jo_hbm, bi_hbm,
    sol, res, hess,
    rs, pw, pd, po, wi, wc, agg, lvl, inv,
    jd, jo, bi, basis, dirs, imgs, near, rem, cvec,
    fld, pkx, hz, hx, pkx12, hz12, hx12,
    invs, invh, rows_src, gath, co_src, co_gath, col_src, peer,
    hbm_sem, halo_send, halo_recv, big_send, big_recv, inv_send, inv_recv,
    row_send, row_recv, co_send, co_recv, peer_send, peer_recv,
):
    comps = rs.shape[0]
    strips = length // LANES
    plane = strips * width
    total = depth * plane
    count = layer_devices * areal_devices
    points = depth * width
    co_rows = invs.shape[0] // points
    aggregates = halves
    g = lax.axis_index("gz")
    e = lax.axis_index("xy")
    me = g * areal_devices + e

    def at(index):
        return {"gz": index // areal_devices, "xy": index % areal_devices}

    pairs = [
        (rs_hbm, rs), (pw_hbm, pw), (pd_hbm, pd), (wi_hbm, wi), (po_hbm, po),
        (lvl_hbm, lvl), (inv_hbm, inv), (agg_hbm, agg), (wc_hbm, wc),
        (jd_hbm, jd), (jo_hbm, jo), (bi_hbm, bi),
    ]
    loads = [
        pltpu.make_async_copy(src, dst, hbm_sem.at[n]) for n, (src, dst) in enumerate(pairs)
    ]
    for load in loads:
        load.start()

    barrier = pltpu.get_barrier_semaphore()

    def greet(step, carry):
        pl.semaphore_signal(
            barrier, inc=1, device_id=at((me + step) % count), device_id_type=MESH
        )
        return carry

    lax.fori_loop(1, count, greet, 0)


    row_at = lax.broadcasted_iota(jnp.int32, (plane, LANES), 0)
    lane_at = lax.broadcasted_iota(jnp.int32, (plane, LANES), 1)
    x_at = row_at % width
    strip_at = row_at // width
    lane_row = lax.broadcasted_iota(jnp.int32, (1, LANES), 1)

    def roll(a, shift, axis):
        size = a.shape[axis]
        shift = shift % size
        return a if shift == 0 else pltpu.roll(a, shift, axis)

    def planes(a):
        return a.reshape(-1, plane, LANES)

    def pack(a, edge):
        p = planes(a).reshape(-1, depth, plane, LANES)
        groups = -(-depth // width)
        out = []
        for group in range(groups):
            acc = jnp.zeros((p.shape[0], plane, LANES), F32)
            for s in range(group * width, min(depth, (group + 1) * width)):
                moved = roll(p[:, s], s % width - edge, 1)
                acc = jnp.where((x_at == s % width)[None], moved, acc)
            out.append(acc)
        return out[0] if groups == 1 else jnp.concatenate(out, axis=1)

    def unpack(b, target):
        parts = []
        for s in range(depth):
            group = s // width
            piece = b[:, group * plane:(group + 1) * plane]
            parts.append(roll(piece, target - s % width, 1))
        return jnp.concatenate(parts, axis=1)

    def tile_rows(mask):
        return jnp.concatenate([mask] * depth, axis=0)[None]

    x_all = tile_rows(x_at)
    def shift_zl(f, h):
        return jnp.concatenate([h, f[:, :-plane]], axis=1) if depth > 1 else h

    def shift_zh(f, h):
        return jnp.concatenate([f[:, plane:], h], axis=1) if depth > 1 else h

    def shift_xl(f, h):
        own = roll(planes(f), 1, 1).reshape(f.shape)
        return jnp.where(x_all == 0, h, own)

    def shift_xh(f, h):
        own = roll(planes(f), -1, 1).reshape(f.shape)
        return jnp.where(x_all == width - 1, h, own)

    def shift_yl(f):
        p = planes(f)
        t = roll(p, 1, 2)
        u = roll(t, width, 1)
        first = (lane_at == 0)[None]
        edge = (strip_at == 0)[None]
        return jnp.where(first, jnp.where(edge, 0.0, u), t).reshape(f.shape)

    def shift_yh(f):
        p = planes(f)
        t = roll(p, -1, 2)
        u = roll(t, -width, 1)
        last = (lane_at == LANES - 1)[None]
        edge = (strip_at == strips - 1)[None]
        return jnp.where(last, jnp.where(edge, 0.0, u), t).reshape(f.shape)

    to = [
        (g < layer_devices - 1, g > 0, {"gz": g + 1, "xy": e}),
        (g > 0, g < layer_devices - 1, {"gz": g - 1, "xy": e}),
        (e < areal_devices - 1, e > 0, {"gz": g, "xy": e + 1}),
        (e > 0, e < areal_devices - 1, {"gz": g, "xy": e - 1}),
    ]

    @pl.when(g == 0)
    def _():
        hz[:, 0] = jnp.zeros(hz.shape[:1] + hz.shape[2:], F32)
        hz12[:, 0] = jnp.zeros(hz12.shape[:1] + hz12.shape[2:], F32)
        invh[0] = jnp.zeros(invh.shape[1:], F32)

    @pl.when(g == layer_devices - 1)
    def _():
        hz[:, 1] = jnp.zeros(hz.shape[:1] + hz.shape[2:], F32)
        hz12[:, 1] = jnp.zeros(hz12.shape[:1] + hz12.shape[2:], F32)
        invh[1] = jnp.zeros(invh.shape[1:], F32)

    @pl.when(e == 0)
    def _():
        hx[:, 0] = jnp.zeros(hx.shape[:1] + hx.shape[2:], F32)
        hx12[:, 0] = jnp.zeros(hx12.shape[:1] + hx12.shape[2:], F32)
        invh[2] = jnp.zeros(invh.shape[1:], F32)

    @pl.when(e == areal_devices - 1)
    def _():
        hx[:, 1] = jnp.zeros(hx.shape[:1] + hx.shape[2:], F32)
        hx12[:, 1] = jnp.zeros(hx12.shape[:1] + hx12.shape[2:], F32)
        invh[3] = jnp.zeros(invh.shape[1:], F32)

    finals = []

    def halo_copies(r):
        srcs = [
            fld.at[r, pl.ds(total - plane, plane)],
            fld.at[r, pl.ds(0, plane)],
            pkx.at[r, 0],
            pkx.at[r, 1],
        ]
        dsts = [hz.at[r, 0], hz.at[r, 1], hx.at[r, 0], hx.at[r, 1]]
        return [
            pltpu.make_async_remote_copy(
                src_ref=srcs[d], dst_ref=dsts[d], send_sem=halo_send.at[r, d],
                recv_sem=halo_recv.at[r, d], device_id=to[d][2], device_id_type=MESH,
            )
            for d in range(4)
        ]

    def big_copies(t):
        srcs = [
            dirs.at[t, :, pl.ds(total - plane, plane)],
            dirs.at[t, :, pl.ds(0, plane)],
            pkx12.at[t, 0],
            pkx12.at[t, 1],
        ]
        dsts = [hz12.at[t, 0], hz12.at[t, 1], hx12.at[t, 0], hx12.at[t, 1]]
        return [
            pltpu.make_async_remote_copy(
                src_ref=srcs[d], dst_ref=dsts[d], send_sem=big_send.at[t, d],
                recv_sem=big_recv.at[t, d], device_id=to[d][2], device_id_type=MESH,
            )
            for d in range(4)
        ]

    def inv_copies():
        return [
            pltpu.make_async_remote_copy(
                src_ref=invs, dst_ref=invh.at[d], send_sem=inv_send.at[d],
                recv_sem=inv_recv.at[d], device_id=to[d][2], device_id_type=MESH,
            )
            for d in range(4)
        ]

    def start_all(copies):
        for d in range(4):
            pl.when(to[d][0])(copies[d].start)
            finals.append((to[d][0], copies[d].wait_send))

    def arrive(copies):
        for d in range(4):
            pl.when(to[d][1])(copies[d].wait_recv)

    def halo_start(r, f):
        fld[r] = f
        pkx[r, 0] = pack(f[None], width - 1)[0]
        pkx[r, 1] = pack(f[None], 0)[0]
        copies = halo_copies(r)
        start_all(copies)
        return copies

    def halo_read(r):
        return (
            hz[r, 0][None], hz[r, 1][None],
            unpack(hx[r, 0][None], 0), unpack(hx[r, 1][None], width - 1),
        )

    def send_all(src, dst, size, send, recv):
        def one(step, carry):
            pltpu.make_async_remote_copy(
                src_ref=src, dst_ref=dst.at[pl.ds(me * size, size)], send_sem=send,
                recv_sem=recv, device_id=at((me + step) % count), device_id_type=MESH,
            ).start()
            return carry

        lax.fori_loop(1, count, one, 0)
        whole = dst.at[pl.ds(0, (count - 1) * size)]
        finals.append((None, pltpu.make_async_copy(whole, whole, send).wait))
        return pltpu.make_async_copy(whole, whole, recv).wait

    def rows_start(r, values):
        row = jnp.zeros((1, LANES), F32)
        for q, value in enumerate(values):
            row = jnp.where(lane_row == q, value, row)
        rows_src[r] = row
        gath[r, pl.ds(me, 1)] = row
        return send_all(rows_src.at[r], gath.at[r], 1, row_send.at[r], row_recv.at[r])

    def rows_read(r, n):
        got = gath[r]
        lanes = lax.broadcasted_iota(jnp.int32, got.shape, 1)
        return [
            jnp.sum(jnp.where(lanes == q, got, 0.0), axis=1, keepdims=True) for q in range(n)
        ]

    def peers_start(r, value):
        col_src[r] = value
        peer[r, g] = value
        for step in range(1, layer_devices):
            pltpu.make_async_remote_copy(
                src_ref=col_src.at[r], dst_ref=peer.at[r, g], send_sem=peer_send.at[r],
                recv_sem=peer_recv.at[r],
                device_id={"gz": (g + step) % layer_devices, "xy": e}, device_id_type=MESH,
            ).start()
        whole = peer.at[r, pl.ds(0, layer_devices - 1)]
        finals.append((None, pltpu.make_async_copy(whole, whole, peer_send.at[r]).wait))
        return pltpu.make_async_copy(whole, whole, peer_recv.at[r]).wait

    def over_planes(f):
        acc = f[0:plane]
        for z in range(1, depth):
            acc = acc + f[z * plane:(z + 1) * plane]
        return acc

    def scalar(a):
        a = jnp.sum(a, axis=0) if a.ndim == 3 else a
        return jnp.sum(jnp.sum(a, axis=0, keepdims=True), axis=1, keepdims=True)

    def ssum(a):
        return jnp.sum(a, axis=0, keepdims=True)

    for load in loads[:5]:
        load.wait()
    diag = pd[...].astype(F32)
    sides = po[...].astype(F32)
    rs_all = rs[...]
    raw_rhs = jnp.sum(pw[...].astype(F32) * rs_all, axis=0)
    raw_guess = raw_rhs / diag
    norm_here = scalar(rs_all * rs_all)
    index = wi[...]
    weight_here = over_planes(index)
    for load in loads[5:9]:
        load.wait()
    nz, nx = inv.shape[2:]
    per = LANES // nx
    inv_z = lax.broadcasted_iota(jnp.int32, (nz, LANES), 0)
    inv_lane = lax.broadcasted_iota(jnp.int32, (nz, LANES), 1)
    for z in range(depth):
        for x in range(width):
            wide = jnp.concatenate([inv[z, x].astype(F32)] * per, axis=1)
            wide = jnp.where(inv_lane // nx == inv_z % per, wide, 0.0)
            point = z * width + x
            for r in range(co_rows):
                invs[pl.ds(point * co_rows + r, 1)] = jnp.sum(
                    wide[r * per:(r + 1) * per], axis=0, keepdims=True
                )
    op = lvl[...].astype(F32)
    op_sum = jnp.sum(op, axis=0)
    op_lane = lax.broadcasted_iota(jnp.int32, op.shape[1:], len(op.shape) - 2)
    op_diag = jnp.zeros(op.shape[1:], F32)
    for a in range(aggregates):
        op_diag = jnp.where(op_lane == a, op[a], op_diag)
    op_row = lax.broadcasted_iota(jnp.int32, (plane, aggregates), 0)
    parts = ([], [])
    for z in range(depth):
        for part, table in zip(parts, (op_sum, op_diag)):
            acc = jnp.zeros((plane, aggregates), F32)
            for x in range(width):
                for b in range(strips):
                    acc = jnp.where(op_row == b * width + x, table[z, x, b:b + 1], acc)
            part.append(acc)
    colsum = jnp.concatenate(parts[0], axis=0)
    codiag = jnp.concatenate(parts[1], axis=0)
    column = (e * width + x_at) * length + strip_at * LANES + lane_at

    pl.semaphore_wait(barrier, count - 1)
    norm_wait = rows_start(0, [norm_here])
    halo_a = halo_start(0, raw_guess)
    inv_all = inv_copies()
    start_all(inv_all)
    weight_wait = peers_start(0, weight_here)

    def tally(w, acc):
        return acc + jnp.where(column == wc[w], 1.0, 0.0)

    wells = lax.fori_loop(0, wc.shape[0], tally, jnp.zeros((plane, LANES), F32))
    wells = jnp.concatenate([wells] * depth, axis=0)
    well_factor = index * wells
    aggs = agg[...]

    def apply_pressure(f, halos):
        f3 = f[None]
        nears = [
            shift_zl(f3, halos[0]), shift_zh(f3, halos[1]),
            shift_xl(f3, halos[2]), shift_xh(f3, halos[3]),
            shift_yl(f3), shift_yh(f3),
        ]
        out = diag * f
        for k in range(6):
            out = out + sides[k] * nears[k][0]
        return out

    def well_start(r, q):
        return peers_start(r, over_planes(index * q))

    norm_wait()
    beta = jnp.sqrt(ssum(rows_read(0, 1)[0]) + EPSILON)
    arrive(halo_a)
    guess_halos = [h / beta for h in halo_read(0)]
    arrive(inv_all)
    basis[0] = rs_all / beta
    rhs = raw_rhs / beta
    guess = raw_guess / beta

    col_weight = None
    hessen = [[jnp.zeros((1, 1), F32) for _ in range(ITERS)] for _ in range(ITERS + 1)]
    lane_all = lax.broadcasted_iota(jnp.int32, (total, aggregates), 1)
    flat_at = (
        lax.broadcasted_iota(jnp.int32, (co_rows, LANES), 0) * LANES
        + lax.broadcasted_iota(jnp.int32, (co_rows, LANES), 1)
    )
    gram = None
    for t in range(ITERS):
        v = basis.at[t]
        rest = rhs - apply_pressure(guess, guess_halos)
        coarse = jnp.zeros((total, aggregates), F32)
        for a in range(aggregates):
            part = jnp.sum(jnp.where(aggs == a, rest, 0.0), axis=1, keepdims=True)
            coarse = jnp.where(lane_all == a, part, coarse)
        coarse_guess = coarse / codiag
        coarse_rest = jnp.sum(coarse - colsum * coarse_guess, axis=1, keepdims=True)
        message = jnp.zeros((co_rows, LANES), F32)
        for z in range(depth):
            part = coarse_rest[z * plane:(z + 1) * plane]
            for x in range(width):
                value = jnp.sum(
                    jnp.where(x_at[:, 0:1] == x, part, 0.0), axis=0, keepdims=True
                )
                spot = (g * depth + z) * (areal_devices * width) + e * width + x
                message = jnp.where(flat_at == spot, value, message)
        message = message.astype(jnp.bfloat16).astype(F32)
        co_src[t] = message
        co_gath[t, pl.ds(me * co_rows, co_rows)] = message
        co_wait = send_all(co_src.at[t], co_gath.at[t], co_rows, co_send.at[t], co_recv.at[t])
        picked = guess
        for a in range(aggregates):
            picked = jnp.where(aggs == a, guess + coarse_guess[:, a:a + 1], picked)
        halo_b = halo_start(1 + 3 * t, picked)
        if t == 0:
            weight_wait()
            col_weight = jnp.sum(peer[0], axis=0)
        b0 = basis[0]
        if t == 0:
            g00 = scalar(b0 * b0)
        else:
            b1 = basis[1]
            g00, g01 = gram[0], scalar(b0 * b1)
            tilt = jnp.where(g00 > TINY, g01 / g00, 0.0)
            perp = b1 - tilt * b0
            cvec[...] = perp
            cc = scalar(perp * perp)
        gram = (g00,)
        co_wait()
        ordered = jnp.sum(co_gath[t].reshape(count, co_rows, LANES), axis=0)

        def coarsest_of(mat):
            prod = mat.reshape(points, co_rows, LANES) * ordered[None]
            return jnp.sum(jnp.sum(prod, axis=1), axis=1, keepdims=True)

        def layer_of(values, z):
            acc = jnp.zeros((plane, LANES), F32)
            for x in range(width):
                at_point = z * width + x
                acc = jnp.where(x_at == x, values[at_point:at_point + 1], acc)
            return acc

        def spread_of(values):
            return jnp.concatenate([layer_of(values, z) for z in range(depth)], axis=0)

        def edge_of(values, x):
            parts = [
                jnp.broadcast_to(
                    values[z * width + x:z * width + x + 1], (plane, LANES)
                )
                for z in range(depth)
            ]
            return jnp.concatenate(parts, axis=0)

        smooth = picked + spread_of(coarsest_of(invs[...]))
        halo_extra = [
            layer_of(coarsest_of(invh[0]), depth - 1),
            layer_of(coarsest_of(invh[1]), 0),
            edge_of(coarsest_of(invh[2]), width - 1),
            edge_of(coarsest_of(invh[3]), 0),
        ]
        arrive(halo_b)
        got = halo_read(1 + 3 * t)
        smooth_halos = [got[d] + halo_extra[d][None] for d in range(4)]
        pressure = smooth + (rhs - apply_pressure(smooth, smooth_halos)) / diag
        halo_d = halo_start(2 + 3 * t, pressure)
        well_wait = well_start(1 + 2 * t, pressure)
        if t == 0:
            for load in loads[9:]:
                load.wait()
        p3 = pressure[None]
        acc = v[...] - jd[:, 0].astype(F32) * p3
        acc = acc - jo[4, :, 0].astype(F32) * shift_yl(p3)
        acc = acc - jo[5, :, 0].astype(F32) * shift_yh(p3)
        arrive(halo_d)
        got = halo_read(2 + 3 * t)
        acc = acc - jo[0, :, 0].astype(F32) * shift_zl(p3, got[0])
        acc = acc - jo[1, :, 0].astype(F32) * shift_zh(p3, got[1])
        acc = acc - jo[2, :, 0].astype(F32) * shift_xl(p3, got[2])
        acc = acc - jo[3, :, 0].astype(F32) * shift_xh(p3, got[3])
        rem[...] = acc

        def well_term(r, q):
            level = jnp.sum(peer[r], axis=0) / col_weight
            return well_factor * (q - jnp.concatenate([level] * depth, axis=0))

        well_wait()
        rem[0] = rem[0] - well_term(1 + 2 * t, pressure)

        def correct(i, carry):
            dirs[t, i] = jnp.sum(bi[i].astype(F32) * rem[...], axis=0)
            return carry

        lax.fori_loop(0, comps, correct, 0)
        head = dirs[t, 0] + pressure
        dirs[t, 0] = head
        d_all = dirs[t]
        pkx12[t, 0] = pack(d_all, width - 1)
        pkx12[t, 1] = pack(d_all, 0)
        big = big_copies(t)
        start_all(big)
        well_wait = well_start(2 + 2 * t, head)
        near[4] = shift_yl(d_all)
        near[5] = shift_yh(d_all)

        def inner(i, carry):
            out = jnp.sum(jd[i].astype(F32) * dirs[t], axis=0)
            for k in (4, 5):
                out = out + jnp.sum(jo[k, i].astype(F32) * near[k], axis=0)
            imgs[t, i] = out
            return carry

        lax.fori_loop(0, comps, inner, 0)
        arrive(big)
        d_all = dirs[t]
        near[0] = shift_zl(d_all, hz12[t, 0])
        near[1] = shift_zh(d_all, hz12[t, 1])
        near[2] = shift_xl(d_all, unpack(hx12[t, 0], 0))
        near[3] = shift_xh(d_all, unpack(hx12[t, 1], width - 1))

        def outer(i, carry):
            out = imgs[t, i]
            for k in range(4):
                out = out + jnp.sum(jo[k, i].astype(F32) * near[k], axis=0)
            imgs[t, i] = out
            return carry

        lax.fori_loop(0, comps, outer, 0)
        well_wait()
        imgs[t, 0] = imgs[t, 0] + well_term(2 + 2 * t, head)
        image = imgs[t]
        b0 = basis[0]
        p0 = scalar(image * b0)
        a0 = jnp.where(g00 > TINY, p0 / g00, 0.0)
        if t == 0:
            left = image - a0 * b0
            rr = scalar(left * left)
            row_wait = rows_start(1, [p0, g00, a0, rr])
            image_guess = jnp.sum(pw[...].astype(F32) * image, axis=0) / diag
            halo_f = halo_start(3, image_guess)
            row_wait()
            q0, gg, aa, ll = rows_read(1, 4)
            h00 = ssum(q0)
            height = jnp.sqrt(ssum(ll + (aa - h00) * (aa - h00) * gg) + EPSILON)
            hessen[0][0] = h00
            hessen[1][0] = height
            next_basis = (image - h00 * b0) / height
            basis[1] = next_basis
            rhs = jnp.sum(pw[...].astype(F32) * next_basis, axis=0)
            guess = rhs / diag
            arrive(halo_f)
            got = halo_read(3)
            guess_halos = [(got[d] - h00 * guess_halos[d]) / height for d in range(4)]
        else:
            perp = cvec[...]
            p1 = scalar(image * basis[1])
            a1 = jnp.where(cc > TINY, scalar(image * perp) / cc, 0.0)
            left = image - a0 * b0 - a1 * perp
            rr = scalar(left * left)
            row_wait = rows_start(2, [p0, p1, g00, tilt, a0, cc, a1, rr])
            row_wait()
            q0, q1, gg, ee, aa0, cc1, aa1, ll = rows_read(2, 8)
            h0 = ssum(q0)
            h1 = ssum(q1)
            d0 = aa0 - h0 - ee * h1
            d1 = aa1 - h1
            hessen[0][1] = h0
            hessen[1][1] = h1
            hessen[2][1] = jnp.sqrt(ssum(ll + d0 * d0 * gg + d1 * d1 * cc1) + EPSILON)

    weights = least_squares(hessen, beta)
    sol[...] = weights[0] * dirs[0] + weights[1] * dirs[1]
    res[...] = rs[...] - (weights[0] * imgs[0] + weights[1] * imgs[1])
    hr = lax.broadcasted_iota(jnp.int32, hess.shape, 0)
    hc = lax.broadcasted_iota(jnp.int32, hess.shape, 1)
    table = jnp.zeros(hess.shape, F32)
    for i in range(ITERS + 1):
        for j in range(ITERS):
            table = jnp.where((hr == j) & (hc == i), hessen[i][j], table)
    hess[...] = table
    for condition, wait in finals:
        if condition is None:
            wait()
        else:
            pl.when(condition)(wait)


def least_squares(hessen, beta):
    upper = [list(line) for line in hessen]
    target = [beta] + [jnp.zeros((1, 1), F32) for line in range(ITERS)]
    rotations = []
    for column in range(ITERS):
        for row, (cosine, sine) in enumerate(rotations):
            first, second = (upper[row][column], upper[row + 1][column])
            upper[row][column] = cosine * first + sine * second
            upper[row + 1][column] = cosine * second - sine * first
        first, second = (upper[column][column], upper[column + 1][column])
        radius = jnp.sqrt(first * first + second * second)
        cosine, sine = (first / radius, second / radius)
        upper[column][column] = radius
        leading = target[column]
        target[column] = cosine * leading
        target[column + 1] = -sine * leading
        rotations.append((cosine, sine))
    weights = [None] * ITERS
    for column in reversed(range(ITERS)):
        total = target[column]
        for later in range(column + 1, ITERS):
            total = total - upper[column][later] * weights[later]
        weights[column] = total / upper[column][column]
    return weights


def to_rows(a):
    depth, width, length = a.shape[-3:]
    lead = a.shape[:-3]
    strips = length // LANES
    a = a.reshape(lead + (depth, width, strips, LANES))
    return jnp.swapaxes(a, -3, -2).reshape(lead + (depth * strips * width, LANES))


def from_rows(a, depth, width, length):
    lead = a.shape[:-2]
    strips = length // LANES
    a = a.reshape(lead + (depth, strips, width, LANES))
    return jnp.swapaxes(a, -3, -2).reshape(lead + (depth, width, length))


def on_device(
    right_side, jac_diag, jac_off, block_inv, press_weight, press_diag, press_off,
    well_index, well_columns, agg_map, level1_op, coarsest_inv,
):
    comps, depth, width, length = right_side.shape
    aggregates = level1_op.shape[0]
    blocks = level1_op.shape[4]
    layer_devices = lax.axis_size("gz")
    areal_devices = lax.axis_size("xy")
    count = layer_devices * areal_devices
    plane = (length // LANES) * width
    total = depth * plane
    points = depth * width
    lvl = level1_op.transpose(0, 2, 3, 4, 1)
    flat = coarsest_inv.shape[2] * coarsest_inv.shape[3]
    co_rows = flat // LANES

    vm = pl.BlockSpec(memory_space=pltpu.VMEM)
    hbm = pl.BlockSpec(memory_space=pltpu.HBM)
    edge_rows = -(-depth // width) * plane
    v = pltpu.VMEM
    dma = pltpu.SemaphoreType.DMA
    scratch = [
        v((comps, total, LANES), F32),
        v((comps, total, LANES), jnp.bfloat16),
        v((total, LANES), jnp.bfloat16),
        v((6, total, LANES), jnp.bfloat16),
        v((total, LANES), F32),
        pltpu.SMEM(well_columns.shape, jnp.int32),
        v((total, LANES), jnp.int32),
        v(lvl.shape, jnp.bfloat16),
        v(coarsest_inv.shape, jnp.bfloat16),
        v((comps, comps, total, LANES), jnp.bfloat16),
        v((6, comps, comps, total, LANES), jnp.bfloat16),
        v((comps, comps, total, LANES), jnp.bfloat16),
        v((ITERS, comps, total, LANES), F32),
        v((ITERS, comps, total, LANES), F32),
        v((ITERS, comps, total, LANES), F32),
        v((6, comps, total, LANES), F32),
        v((comps, total, LANES), F32),
        v((comps, total, LANES), F32),
        v((ROUNDS, total, LANES), F32),
        v((ROUNDS, 2, edge_rows, LANES), F32),
        v((ROUNDS, 2, plane, LANES), F32),
        v((ROUNDS, 2, edge_rows, LANES), F32),
        v((ITERS, 2, comps, edge_rows, LANES), F32),
        v((ITERS, 2, comps, plane, LANES), F32),
        v((ITERS, 2, comps, edge_rows, LANES), F32),
        v((points * co_rows, LANES), F32),
        v((4, points * co_rows, LANES), F32),
        v((3, 1, LANES), F32),
        v((3, count, LANES), F32),
        v((ITERS, co_rows, LANES), F32),
        v((ITERS, count * co_rows, LANES), F32),
        v((5, plane, LANES), F32),
        v((5, layer_devices, plane, LANES), F32),
        dma((12,)),
        dma((ROUNDS, 4)), dma((ROUNDS, 4)),
        dma((ITERS, 4)), dma((ITERS, 4)),
        dma((4,)), dma((4,)),
        dma((3,)), dma((3,)),
        dma((ITERS,)), dma((ITERS,)),
        dma((5,)), dma((5,)),
    ]
    body = functools.partial(
        kernel, depth, width, length, layer_devices, areal_devices, aggregates
    )
    sol, res, hess = pl.pallas_call(
        body,
        out_shape=(
            jax.ShapeDtypeStruct((comps, total, LANES), F32),
            jax.ShapeDtypeStruct((comps, total, LANES), F32),
            jax.ShapeDtypeStruct((ITERS, ITERS + 1), F32),
        ),
        in_specs=[hbm] * 12,
        out_specs=(vm, vm, vm),
        scratch_shapes=scratch,
        compiler_params=pltpu.CompilerParams(
            collective_id=0, has_side_effects=True, vmem_limit_bytes=63 * 1024 * 1024
        ),
    )(
        to_rows(right_side), to_rows(press_weight), to_rows(press_diag), to_rows(press_off),
        to_rows(well_index), well_columns, to_rows(agg_map), lvl, coarsest_inv,
        to_rows(jac_diag), to_rows(jac_off), to_rows(block_inv),
    )
    return (
        from_rows(sol, depth, width, length),
        from_rows(res, depth, width, length),
        hess.T,
    )


def solution(mesh):
    in_specs = (
        P(None, "gz", "xy", None),
        P(None, None, "gz", "xy", None),
        P(None, None, None, "gz", "xy", None),
        P(None, None, "gz", "xy", None),
        P(None, "gz", "xy", None),
        P("gz", "xy", None),
        P(None, "gz", "xy", None),
        P("gz", "xy", None),
        P(),
        P("gz", "xy", None),
        P(None, None, "gz", "xy", None),
        P("gz", "xy", None, None),
    )
    out_specs = (P(None, "gz", "xy", None), P(None, "gz", "xy", None), P())
    return jax.shard_map(
        on_device, mesh=mesh, in_specs=in_specs, out_specs=out_specs, check_vma=False
    )
```

```python
import functools

import jax
import jax.numpy as jnp
from jax import lax
from jax.experimental import pallas as pl
from jax.experimental.pallas import tpu as pltpu
from jax.sharding import PartitionSpec as P

ITERS = 2
EPSILON = 1e-06
LANES = 128
TINY = 1e-30
F32 = jnp.float32
MESH = pl.DeviceIdType.MESH
ROUNDS = 6


def kernel(
    depth, width, length, layer_devices, areal_devices, halves,
    rs_hbm, pw_hbm, pd_hbm, po_hbm, wi_hbm, wc_hbm, agg_hbm, lvl_hbm, inv_hbm,
    jd_hbm, jo_hbm, bi_hbm,
    sol, res, hess,
    rs, pw, pd, po, wi, wc, agg, lvl, inv,
    jd, jo, bi, basis, dirs, imgs, near, rem, cvec,
    fld, pkx, hz, hx, pkx12, hz12, hx12,
    invs, invh, rows_src, gath, co_src, co_gath, col_src, peer,
    hbm_sem, halo_send, halo_recv, big_send, big_recv, inv_send, inv_recv,
    row_send, row_recv, co_send, co_recv, peer_send, peer_recv,
):
    comps = rs.shape[0]
    strips = length // LANES
    plane = strips * width
    total = depth * plane
    count = layer_devices * areal_devices
    points = depth * width
    co_rows = invs.shape[0] // points
    aggregates = halves
    g = lax.axis_index("gz")
    e = lax.axis_index("xy")
    me = g * areal_devices + e

    def at(index):
        return {"gz": index // areal_devices, "xy": index % areal_devices}

    pairs = [
        (rs_hbm, rs), (pw_hbm, pw), (pd_hbm, pd), (wi_hbm, wi), (po_hbm, po),
        (lvl_hbm, lvl), (inv_hbm, inv), (agg_hbm, agg), (wc_hbm, wc),
        (jd_hbm, jd), (jo_hbm, jo), (bi_hbm, bi),
    ]
    loads = [
        pltpu.make_async_copy(src, dst, hbm_sem.at[n]) for n, (src, dst) in enumerate(pairs)
    ]
    for load in loads:
        load.start()

    barrier = pltpu.get_barrier_semaphore()

    def greet(step, carry):
        pl.semaphore_signal(
            barrier, inc=1, device_id=at((me + step) % count), device_id_type=MESH
        )
        return carry

    lax.fori_loop(1, count, greet, 0)


    row_at = lax.broadcasted_iota(jnp.int32, (plane, LANES), 0)
    lane_at = lax.broadcasted_iota(jnp.int32, (plane, LANES), 1)
    x_at = row_at % width
    strip_at = row_at // width
    lane_row = lax.broadcasted_iota(jnp.int32, (1, LANES), 1)

    def roll(a, shift, axis):
        size = a.shape[axis]
        shift = shift % size
        return a if shift == 0 else pltpu.roll(a, shift, axis)

    def planes(a):
        return a.reshape(-1, plane, LANES)

    def pack(a, edge):
        p = planes(a).reshape(-1, depth, plane, LANES)
        groups = -(-depth // width)
        out = []
        for group in range(groups):
            acc = jnp.zeros((p.shape[0], plane, LANES), F32)
            for s in range(group * width, min(depth, (group + 1) * width)):
                moved = roll(p[:, s], s % width - edge, 1)
                acc = jnp.where((x_at == s % width)[None], moved, acc)
            out.append(acc)
        return out[0] if groups == 1 else jnp.concatenate(out, axis=1)

    def unpack(b, target):
        parts = []
        for s in range(depth):
            group = s // width
            piece = b[:, group * plane:(group + 1) * plane]
            parts.append(roll(piece, target - s % width, 1))
        return jnp.concatenate(parts, axis=1)

    def tile_rows(mask):
        return jnp.concatenate([mask] * depth, axis=0)[None]

    x_all = tile_rows(x_at)
    def shift_zl(f, h):
        return jnp.concatenate([h, f[:, :-plane]], axis=1) if depth > 1 else h

    def shift_zh(f, h):
        return jnp.concatenate([f[:, plane:], h], axis=1) if depth > 1 else h

    def shift_xl(f, h):
        own = roll(planes(f), 1, 1).reshape(f.shape)
        return jnp.where(x_all == 0, h, own)

    def shift_xh(f, h):
        own = roll(planes(f), -1, 1).reshape(f.shape)
        return jnp.where(x_all == width - 1, h, own)

    def shift_yl(f):
        p = planes(f)
        t = roll(p, 1, 2)
        u = roll(t, width, 1)
        first = (lane_at == 0)[None]
        edge = (strip_at == 0)[None]
        return jnp.where(first, jnp.where(edge, 0.0, u), t).reshape(f.shape)

    def shift_yh(f):
        p = planes(f)
        t = roll(p, -1, 2)
        u = roll(t, -width, 1)
        last = (lane_at == LANES - 1)[None]
        edge = (strip_at == strips - 1)[None]
        return jnp.where(last, jnp.where(edge, 0.0, u), t).reshape(f.shape)

    to = [
        (g < layer_devices - 1, g > 0, {"gz": g + 1, "xy": e}),
        (g > 0, g < layer_devices - 1, {"gz": g - 1, "xy": e}),
        (e < areal_devices - 1, e > 0, {"gz": g, "xy": e + 1}),
        (e > 0, e < areal_devices - 1, {"gz": g, "xy": e - 1}),
    ]

    @pl.when(g == 0)
    def _():
        hz[:, 0] = jnp.zeros(hz.shape[:1] + hz.shape[2:], F32)
        hz12[:, 0] = jnp.zeros(hz12.shape[:1] + hz12.shape[2:], F32)
        invh[0] = jnp.zeros(invh.shape[1:], F32)

    @pl.when(g == layer_devices - 1)
    def _():
        hz[:, 1] = jnp.zeros(hz.shape[:1] + hz.shape[2:], F32)
        hz12[:, 1] = jnp.zeros(hz12.shape[:1] + hz12.shape[2:], F32)
        invh[1] = jnp.zeros(invh.shape[1:], F32)

    @pl.when(e == 0)
    def _():
        hx[:, 0] = jnp.zeros(hx.shape[:1] + hx.shape[2:], F32)
        hx12[:, 0] = jnp.zeros(hx12.shape[:1] + hx12.shape[2:], F32)
        invh[2] = jnp.zeros(invh.shape[1:], F32)

    @pl.when(e == areal_devices - 1)
    def _():
        hx[:, 1] = jnp.zeros(hx.shape[:1] + hx.shape[2:], F32)
        hx12[:, 1] = jnp.zeros(hx12.shape[:1] + hx12.shape[2:], F32)
        invh[3] = jnp.zeros(invh.shape[1:], F32)

    finals = []

    def halo_copies(r):
        srcs = [
            fld.at[r, pl.ds(total - plane, plane)],
            fld.at[r, pl.ds(0, plane)],
            pkx.at[r, 0],
            pkx.at[r, 1],
        ]
        dsts = [hz.at[r, 0], hz.at[r, 1], hx.at[r, 0], hx.at[r, 1]]
        return [
            pltpu.make_async_remote_copy(
                src_ref=srcs[d], dst_ref=dsts[d], send_sem=halo_send.at[r, d],
                recv_sem=halo_recv.at[r, d], device_id=to[d][2], device_id_type=MESH,
            )
            for d in range(4)
        ]

    def big_copies(t):
        srcs = [
            dirs.at[t, :, pl.ds(total - plane, plane)],
            dirs.at[t, :, pl.ds(0, plane)],
            pkx12.at[t, 0],
            pkx12.at[t, 1],
        ]
        dsts = [hz12.at[t, 0], hz12.at[t, 1], hx12.at[t, 0], hx12.at[t, 1]]
        return [
            pltpu.make_async_remote_copy(
                src_ref=srcs[d], dst_ref=dsts[d], send_sem=big_send.at[t, d],
                recv_sem=big_recv.at[t, d], device_id=to[d][2], device_id_type=MESH,
            )
            for d in range(4)
        ]

    def inv_copies():
        return [
            pltpu.make_async_remote_copy(
                src_ref=invs, dst_ref=invh.at[d], send_sem=inv_send.at[d],
                recv_sem=inv_recv.at[d], device_id=to[d][2], device_id_type=MESH,
            )
            for d in range(4)
        ]

    def start_all(copies):
        for d in range(4):
            pl.when(to[d][0])(copies[d].start)
            finals.append((to[d][0], copies[d].wait_send))

    def arrive(copies):
        for d in range(4):
            pl.when(to[d][1])(copies[d].wait_recv)

    def halo_start(r, f):
        fld[r] = f
        pkx[r, 0] = pack(f[None], width - 1)[0]
        pkx[r, 1] = pack(f[None], 0)[0]
        copies = halo_copies(r)
        start_all(copies)
        return copies

    def halo_read(r):
        return (
            hz[r, 0][None], hz[r, 1][None],
            unpack(hx[r, 0][None], 0), unpack(hx[r, 1][None], width - 1),
        )

    def send_all(src, dst, size, send, recv):
        def one(step, carry):
            pltpu.make_async_remote_copy(
                src_ref=src, dst_ref=dst.at[pl.ds(me * size, size)], send_sem=send,
                recv_sem=recv, device_id=at((me + step) % count), device_id_type=MESH,
            ).start()
            return carry

        lax.fori_loop(1, count, one, 0)
        whole = dst.at[pl.ds(0, (count - 1) * size)]
        finals.append((None, pltpu.make_async_copy(whole, whole, send).wait))
        return pltpu.make_async_copy(whole, whole, recv).wait

    def rows_start(r, values):
        row = jnp.zeros((1, LANES), F32)
        for q, value in enumerate(values):
            row = jnp.where(lane_row == q, value, row)
        rows_src[r] = row
        gath[r, pl.ds(me, 1)] = row
        return send_all(rows_src.at[r], gath.at[r], 1, row_send.at[r], row_recv.at[r])

    def rows_read(r, n):
        got = gath[r]
        lanes = lax.broadcasted_iota(jnp.int32, got.shape, 1)
        return [
            jnp.sum(jnp.where(lanes == q, got, 0.0), axis=1, keepdims=True) for q in range(n)
        ]

    def peers_start(r, value):
        col_src[r] = value
        peer[r, g] = value
        for step in range(1, layer_devices):
            pltpu.make_async_remote_copy(
                src_ref=col_src.at[r], dst_ref=peer.at[r, g], send_sem=peer_send.at[r],
                recv_sem=peer_recv.at[r],
                device_id={"gz": (g + step) % layer_devices, "xy": e}, device_id_type=MESH,
            ).start()
        whole = peer.at[r, pl.ds(0, layer_devices - 1)]
        finals.append((None, pltpu.make_async_copy(whole, whole, peer_send.at[r]).wait))
        return pltpu.make_async_copy(whole, whole, peer_recv.at[r]).wait

    def over_planes(f):
        acc = f[0:plane]
        for z in range(1, depth):
            acc = acc + f[z * plane:(z + 1) * plane]
        return acc

    def scalar(a):
        a = jnp.sum(a, axis=0) if a.ndim == 3 else a
        return jnp.sum(jnp.sum(a, axis=0, keepdims=True), axis=1, keepdims=True)

    def ssum(a):
        return jnp.sum(a, axis=0, keepdims=True)

    for load in loads[:5]:
        load.wait()
    diag = pd[...].astype(F32)
    sides = po[...].astype(F32)
    rs_all = rs[...]
    raw_rhs = jnp.sum(pw[...].astype(F32) * rs_all, axis=0)
    raw_guess = raw_rhs / diag
    norm_here = scalar(rs_all * rs_all)
    index = wi[...]
    weight_here = over_planes(index)
    for load in loads[5:9]:
        load.wait()
    nz, nx = inv.shape[2:]
    per = LANES // nx
    inv_z = lax.broadcasted_iota(jnp.int32, (nz, LANES), 0)
    inv_lane = lax.broadcasted_iota(jnp.int32, (nz, LANES), 1)
    for z in range(depth):
        for x in range(width):
            wide = jnp.concatenate([inv[z, x].astype(F32)] * per, axis=1)
            wide = jnp.where(inv_lane // nx == inv_z % per, wide, 0.0)
            point = z * width + x
            for r in range(co_rows):
                invs[pl.ds(point * co_rows + r, 1)] = jnp.sum(
                    wide[r * per:(r + 1) * per], axis=0, keepdims=True
                )
    op = lvl[...].astype(F32)
    op_sum = jnp.sum(op, axis=0)
    op_lane = lax.broadcasted_iota(jnp.int32, op.shape[1:], len(op.shape) - 2)
    op_diag = jnp.zeros(op.shape[1:], F32)
    for a in range(aggregates):
        op_diag = jnp.where(op_lane == a, op[a], op_diag)
    op_row = lax.broadcasted_iota(jnp.int32, (plane, aggregates), 0)
    parts = ([], [])
    for z in range(depth):
        for part, table in zip(parts, (op_sum, op_diag)):
            acc = jnp.zeros((plane, aggregates), F32)
            for x in range(width):
                for b in range(strips):
                    acc = jnp.where(op_row == b * width + x, table[z, x, b:b + 1], acc)
            part.append(acc)
    colsum = jnp.concatenate(parts[0], axis=0)
    codiag = jnp.concatenate(parts[1], axis=0)
    column = (e * width + x_at) * length + strip_at * LANES + lane_at

    pl.semaphore_wait(barrier, count - 1)
    norm_wait = rows_start(0, [norm_here])
    halo_a = halo_start(0, raw_guess)
    inv_all = inv_copies()
    start_all(inv_all)
    weight_wait = peers_start(0, weight_here)

    def tally(w, acc):
        return acc + jnp.where(column == wc[w], 1.0, 0.0)

    wells = lax.fori_loop(0, wc.shape[0], tally, jnp.zeros((plane, LANES), F32))
    wells = jnp.concatenate([wells] * depth, axis=0)
    well_factor = index * wells
    aggs = agg[...]

    def apply_pressure(f, halos):
        f3 = f[None]
        nears = [
            shift_zl(f3, halos[0]), shift_zh(f3, halos[1]),
            shift_xl(f3, halos[2]), shift_xh(f3, halos[3]),
            shift_yl(f3), shift_yh(f3),
        ]
        out = diag * f
        for k in range(6):
            out = out + sides[k] * nears[k][0]
        return out

    def well_start(r, q):
        return peers_start(r, over_planes(index * q))

    norm_wait()
    beta = jnp.sqrt(ssum(rows_read(0, 1)[0]) + EPSILON)
    arrive(halo_a)
    guess_halos = [h / beta for h in halo_read(0)]
    arrive(inv_all)
    basis[0] = rs_all / beta
    rhs = raw_rhs / beta
    guess = raw_guess / beta

    col_weight = None
    hessen = [[jnp.zeros((1, 1), F32) for _ in range(ITERS)] for _ in range(ITERS + 1)]
    lane_all = lax.broadcasted_iota(jnp.int32, (total, aggregates), 1)
    flat_at = (
        lax.broadcasted_iota(jnp.int32, (co_rows, LANES), 0) * LANES
        + lax.broadcasted_iota(jnp.int32, (co_rows, LANES), 1)
    )
    gram = None
    for t in range(ITERS):
        v = basis.at[t]
        rest = rhs - apply_pressure(guess, guess_halos)
        coarse = jnp.zeros((total, aggregates), F32)
        for a in range(aggregates):
            part = jnp.sum(jnp.where(aggs == a, rest, 0.0), axis=1, keepdims=True)
            coarse = jnp.where(lane_all == a, part, coarse)
        coarse_guess = coarse / codiag
        coarse_rest = jnp.sum(coarse - colsum * coarse_guess, axis=1, keepdims=True)
        message = jnp.zeros((co_rows, LANES), F32)
        for z in range(depth):
            part = coarse_rest[z * plane:(z + 1) * plane]
            for x in range(width):
                value = jnp.sum(
                    jnp.where(x_at[:, 0:1] == x, part, 0.0), axis=0, keepdims=True
                )
                spot = (g * depth + z) * (areal_devices * width) + e * width + x
                message = jnp.where(flat_at == spot, value, message)
        message = message.astype(jnp.bfloat16).astype(F32)
        co_src[t] = message
        co_gath[t, pl.ds(me * co_rows, co_rows)] = message
        co_wait = send_all(co_src.at[t], co_gath.at[t], co_rows, co_send.at[t], co_recv.at[t])
        picked = guess
        for a in range(aggregates):
            picked = jnp.where(aggs == a, guess + coarse_guess[:, a:a + 1], picked)
        halo_b = halo_start(1 + 3 * t, picked)
        if t == 0:
            weight_wait()
            col_weight = jnp.sum(peer[0], axis=0)
        b0 = basis[0]
        if t == 0:
            g00 = scalar(b0 * b0)
        else:
            b1 = basis[1]
            g00, g01 = gram[0], scalar(b0 * b1)
            tilt = jnp.where(g00 > TINY, g01 / g00, 0.0)
            perp = b1 - tilt * b0
            cvec[...] = perp
            cc = scalar(perp * perp)
        gram = (g00,)
        co_wait()
        ordered = jnp.sum(co_gath[t].reshape(count, co_rows, LANES), axis=0)

        def coarsest_of(mat):
            prod = mat.reshape(points, co_rows, LANES) * ordered[None]
            return jnp.sum(jnp.sum(prod, axis=1), axis=1, keepdims=True)

        def layer_of(values, z):
            acc = jnp.zeros((plane, LANES), F32)
            for x in range(width):
                at_point = z * width + x
                acc = jnp.where(x_at == x, values[at_point:at_point + 1], acc)
            return acc

        def spread_of(values):
            return jnp.concatenate([layer_of(values, z) for z in range(depth)], axis=0)

        def edge_of(values, x):
            parts = [
                jnp.broadcast_to(
                    values[z * width + x:z * width + x + 1], (plane, LANES)
                )
                for z in range(depth)
            ]
            return jnp.concatenate(parts, axis=0)

        smooth = picked + spread_of(coarsest_of(invs[...]))
        halo_extra = [
            layer_of(coarsest_of(invh[0]), depth - 1),
            layer_of(coarsest_of(invh[1]), 0),
            edge_of(coarsest_of(invh[2]), width - 1),
            edge_of(coarsest_of(invh[3]), 0),
        ]
        arrive(halo_b)
        got = halo_read(1 + 3 * t)
        smooth_halos = [got[d] + halo_extra[d][None] for d in range(4)]
        pressure = smooth + (rhs - apply_pressure(smooth, smooth_halos)) / diag
        well_wait = well_start(1 + 2 * t, pressure)
        halo_d = halo_start(2 + 3 * t, pressure)
        if t == 0:
            for load in loads[9:]:
                load.wait()
        p3 = pressure[None]
        acc = v[...] - jd[:, 0].astype(F32) * p3
        acc = acc - jo[4, :, 0].astype(F32) * shift_yl(p3)
        acc = acc - jo[5, :, 0].astype(F32) * shift_yh(p3)
        arrive(halo_d)
        got = halo_read(2 + 3 * t)
        acc = acc - jo[0, :, 0].astype(F32) * shift_zl(p3, got[0])
        acc = acc - jo[1, :, 0].astype(F32) * shift_zh(p3, got[1])
        acc = acc - jo[2, :, 0].astype(F32) * shift_xl(p3, got[2])
        acc = acc - jo[3, :, 0].astype(F32) * shift_xh(p3, got[3])
        rem[...] = acc

        def well_term(r, q):
            level = jnp.sum(peer[r], axis=0) / col_weight
            return well_factor * (q - jnp.concatenate([level] * depth, axis=0))

        well_wait()
        rem[0] = rem[0] - well_term(1 + 2 * t, pressure)

        def correct(i, carry):
            dirs[t, i] = jnp.sum(bi[i].astype(F32) * rem[...], axis=0)
            return carry

        lax.fori_loop(0, comps, correct, 0)
        head = dirs[t, 0] + pressure
        dirs[t, 0] = head
        well_wait = well_start(2 + 2 * t, head)
        d_all = dirs[t]
        pkx12[t, 0] = pack(d_all, width - 1)
        pkx12[t, 1] = pack(d_all, 0)
        big = big_copies(t)
        start_all(big)
        near[4] = shift_yl(d_all)
        near[5] = shift_yh(d_all)

        def inner(i, carry):
            out = jnp.sum(jd[i].astype(F32) * dirs[t], axis=0)
            for k in (4, 5):
                out = out + jnp.sum(jo[k, i].astype(F32) * near[k], axis=0)
            imgs[t, i] = out
            return carry

        lax.fori_loop(0, comps, inner, 0)
        arrive(big)
        d_all = dirs[t]
        near[0] = shift_zl(d_all, hz12[t, 0])
        near[1] = shift_zh(d_all, hz12[t, 1])
        near[2] = shift_xl(d_all, unpack(hx12[t, 0], 0))
        near[3] = shift_xh(d_all, unpack(hx12[t, 1], width - 1))

        def outer(i, carry):
            out = imgs[t, i]
            for k in range(4):
                out = out + jnp.sum(jo[k, i].astype(F32) * near[k], axis=0)
            imgs[t, i] = out
            return carry

        lax.fori_loop(0, comps, outer, 0)
        well_wait()
        imgs[t, 0] = imgs[t, 0] + well_term(2 + 2 * t, head)
        image = imgs[t]
        b0 = basis[0]
        p0 = scalar(image * b0)
        a0 = jnp.where(g00 > TINY, p0 / g00, 0.0)
        if t == 0:
            left = image - a0 * b0
            rr = scalar(left * left)
            row_wait = rows_start(1, [p0, g00, a0, rr])
            image_guess = jnp.sum(pw[...].astype(F32) * image, axis=0) / diag
            halo_f = halo_start(3, image_guess)
            row_wait()
            q0, gg, aa, ll = rows_read(1, 4)
            h00 = ssum(q0)
            height = jnp.sqrt(ssum(ll + (aa - h00) * (aa - h00) * gg) + EPSILON)
            hessen[0][0] = h00
            hessen[1][0] = height
            next_basis = (image - h00 * b0) / height
            basis[1] = next_basis
            rhs = jnp.sum(pw[...].astype(F32) * next_basis, axis=0)
            guess = rhs / diag
            arrive(halo_f)
            got = halo_read(3)
            guess_halos = [(got[d] - h00 * guess_halos[d]) / height for d in range(4)]
        else:
            perp = cvec[...]
            p1 = scalar(image * basis[1])
            a1 = jnp.where(cc > TINY, scalar(image * perp) / cc, 0.0)
            left = image - a0 * b0 - a1 * perp
            rr = scalar(left * left)
            row_wait = rows_start(2, [p0, p1, g00, tilt, a0, cc, a1, rr])
            row_wait()
            q0, q1, gg, ee, aa0, cc1, aa1, ll = rows_read(2, 8)
            h0 = ssum(q0)
            h1 = ssum(q1)
            d0 = aa0 - h0 - ee * h1
            d1 = aa1 - h1
            hessen[0][1] = h0
            hessen[1][1] = h1
            hessen[2][1] = jnp.sqrt(ssum(ll + d0 * d0 * gg + d1 * d1 * cc1) + EPSILON)

    weights = least_squares(hessen, beta)
    sol[...] = weights[0] * dirs[0] + weights[1] * dirs[1]
    res[...] = rs[...] - (weights[0] * imgs[0] + weights[1] * imgs[1])
    hr = lax.broadcasted_iota(jnp.int32, hess.shape, 0)
    hc = lax.broadcasted_iota(jnp.int32, hess.shape, 1)
    table = jnp.zeros(hess.shape, F32)
    for i in range(ITERS + 1):
        for j in range(ITERS):
            table = jnp.where((hr == j) & (hc == i), hessen[i][j], table)
    hess[...] = table
    for condition, wait in finals:
        if condition is None:
            wait()
        else:
            pl.when(condition)(wait)


def least_squares(hessen, beta):
    upper = [list(line) for line in hessen]
    target = [beta] + [jnp.zeros((1, 1), F32) for line in range(ITERS)]
    rotations = []
    for column in range(ITERS):
        for row, (cosine, sine) in enumerate(rotations):
            first, second = (upper[row][column], upper[row + 1][column])
            upper[row][column] = cosine * first + sine * second
            upper[row + 1][column] = cosine * second - sine * first
        first, second = (upper[column][column], upper[column + 1][column])
        radius = jnp.sqrt(first * first + second * second)
        cosine, sine = (first / radius, second / radius)
        upper[column][column] = radius
        leading = target[column]
        target[column] = cosine * leading
        target[column + 1] = -sine * leading
        rotations.append((cosine, sine))
    weights = [None] * ITERS
    for column in reversed(range(ITERS)):
        total = target[column]
        for later in range(column + 1, ITERS):
            total = total - upper[column][later] * weights[later]
        weights[column] = total / upper[column][column]
    return weights


def to_rows(a):
    depth, width, length = a.shape[-3:]
    lead = a.shape[:-3]
    strips = length // LANES
    a = a.reshape(lead + (depth, width, strips, LANES))
    return jnp.swapaxes(a, -3, -2).reshape(lead + (depth * strips * width, LANES))


def from_rows(a, depth, width, length):
    lead = a.shape[:-2]
    strips = length // LANES
    a = a.reshape(lead + (depth, strips, width, LANES))
    return jnp.swapaxes(a, -3, -2).reshape(lead + (depth, width, length))


def on_device(
    right_side, jac_diag, jac_off, block_inv, press_weight, press_diag, press_off,
    well_index, well_columns, agg_map, level1_op, coarsest_inv,
):
    comps, depth, width, length = right_side.shape
    aggregates = level1_op.shape[0]
    blocks = level1_op.shape[4]
    layer_devices = lax.axis_size("gz")
    areal_devices = lax.axis_size("xy")
    count = layer_devices * areal_devices
    plane = (length // LANES) * width
    total = depth * plane
    points = depth * width
    lvl = level1_op.transpose(0, 2, 3, 4, 1)
    flat = coarsest_inv.shape[2] * coarsest_inv.shape[3]
    co_rows = flat // LANES

    vm = pl.BlockSpec(memory_space=pltpu.VMEM)
    hbm = pl.BlockSpec(memory_space=pltpu.HBM)
    edge_rows = -(-depth // width) * plane
    v = pltpu.VMEM
    dma = pltpu.SemaphoreType.DMA
    scratch = [
        v((comps, total, LANES), F32),
        v((comps, total, LANES), jnp.bfloat16),
        v((total, LANES), jnp.bfloat16),
        v((6, total, LANES), jnp.bfloat16),
        v((total, LANES), F32),
        pltpu.SMEM(well_columns.shape, jnp.int32),
        v((total, LANES), jnp.int32),
        v(lvl.shape, jnp.bfloat16),
        v(coarsest_inv.shape, jnp.bfloat16),
        v((comps, comps, total, LANES), jnp.bfloat16),
        v((6, comps, comps, total, LANES), jnp.bfloat16),
        v((comps, comps, total, LANES), jnp.bfloat16),
        v((ITERS, comps, total, LANES), F32),
        v((ITERS, comps, total, LANES), F32),
        v((ITERS, comps, total, LANES), F32),
        v((6, comps, total, LANES), F32),
        v((comps, total, LANES), F32),
        v((comps, total, LANES), F32),
        v((ROUNDS, total, LANES), F32),
        v((ROUNDS, 2, edge_rows, LANES), F32),
        v((ROUNDS, 2, plane, LANES), F32),
        v((ROUNDS, 2, edge_rows, LANES), F32),
        v((ITERS, 2, comps, edge_rows, LANES), F32),
        v((ITERS, 2, comps, plane, LANES), F32),
        v((ITERS, 2, comps, edge_rows, LANES), F32),
        v((points * co_rows, LANES), F32),
        v((4, points * co_rows, LANES), F32),
        v((3, 1, LANES), F32),
        v((3, count, LANES), F32),
        v((ITERS, co_rows, LANES), F32),
        v((ITERS, count * co_rows, LANES), F32),
        v((5, plane, LANES), F32),
        v((5, layer_devices, plane, LANES), F32),
        dma((12,)),
        dma((ROUNDS, 4)), dma((ROUNDS, 4)),
        dma((ITERS, 4)), dma((ITERS, 4)),
        dma((4,)), dma((4,)),
        dma((3,)), dma((3,)),
        dma((ITERS,)), dma((ITERS,)),
        dma((5,)), dma((5,)),
    ]
    body = functools.partial(
        kernel, depth, width, length, layer_devices, areal_devices, aggregates
    )
    sol, res, hess = pl.pallas_call(
        body,
        out_shape=(
            v((comps, total, LANES), F32),
            v((comps, total, LANES), F32),
            v((ITERS, ITERS + 1), F32),
        ),
        in_specs=[hbm] * 12,
        out_specs=(vm, vm, vm),
        scratch_shapes=scratch,
        compiler_params=pltpu.CompilerParams(
            collective_id=0, has_side_effects=True, vmem_limit_bytes=60 * 1024 * 1024
        ),
    )(
        to_rows(right_side), to_rows(press_weight), to_rows(press_diag), to_rows(press_off),
        to_rows(well_index), well_columns, to_rows(agg_map), lvl, coarsest_inv,
        to_rows(jac_diag), to_rows(jac_off), to_rows(block_inv),
    )
    return (
        from_rows(sol, depth, width, length),
        from_rows(res, depth, width, length),
        hess.T,
    )


def solution(mesh):
    in_specs = (
        P(None, "gz", "xy", None),
        P(None, None, "gz", "xy", None),
        P(None, None, None, "gz", "xy", None),
        P(None, None, "gz", "xy", None),
        P(None, "gz", "xy", None),
        P("gz", "xy", None),
        P(None, "gz", "xy", None),
        P("gz", "xy", None),
        P(),
        P("gz", "xy", None),
        P(None, None, "gz", "xy", None),
        P("gz", "xy", None, None),
    )
    out_specs = (P(None, "gz", "xy", None), P(None, "gz", "xy", None), P())
    return jax.shard_map(
        on_device, mesh=mesh, in_specs=in_specs, out_specs=out_specs, check_vma=False
    )
```
